128 devices in a mesh: grp: 8 (over x_hi, y), tp: 16 (over x_lo, z, core).
Axes of the slice: x: 4 (x_hi: 2, x_lo: 2; x = x_hi * 2 + x_lo), y: 4, z: 4, core: 2. Of those that a mesh axis runs over, the one named last changes fastest.
Arguments:
- tokens: bfloat16 [16384, 2560], P(('grp', 'tp')), may hold values from -6 to 6
- grad_out: bfloat16 [16384, 2560], P(('grp', 'tp')), may hold values from -6 to 6
- route_score: float32 [16384], P(('grp', 'tp')), may hold values from 0.2 to 1
- expert_ids: int32 [16384], P(('grp', 'tp')), may hold values from 0 to 127, as said below
- slots: int32 [16384], P(('grp', 'tp')), may hold values from 0 to 5, as said below
- counts: int32 [128, 8], P(('grp', 'tp')), may hold values from 0 to 4, as said below
- shared_gate_pre: bfloat16 [16384, 4096], P('grp', 'tp'), may hold values from -6 to 6
- shared_up_pre: bfloat16 [16384, 4096], P('grp', 'tp'), may hold values from -6 to 6
- shared_w_gate: bfloat16 [2560, 4096], P(None, 'tp'), may hold values from -0.125 to 0.125
- shared_w_up: bfloat16 [2560, 4096], P(None, 'tp'), may hold values from -0.125 to 0.125
- shared_w_down: bfloat16 [4096, 2560], P('tp'), may hold values from -0.09375 to 0.09375
- w_gate: bfloat16 [8, 2560, 4096], P('grp', None, 'tp'), may hold values from -0.125 to 0.125
- w_up: bfloat16 [8, 2560, 4096], P('grp', None, 'tp'), may hold values from -0.125 to 0.125
- w_down: bfloat16 [8, 4096, 2560], P('grp', 'tp'), may hold values from -0.09375 to 0.09375
Outputs:
- grad_tokens: bfloat16 [16384, 2560], P(('grp', 'tp'))
- grad_score: float32 [16384], P(('grp', 'tp'))
- grad_shared_gate: bfloat16 [2560, 4096], P('grp', 'tp')
- grad_shared_up: bfloat16 [2560, 4096], P('grp', 'tp')
- grad_shared_down: bfloat16 [4096, 2560], P('tp', 'grp')
- grad_gate: bfloat16 [8, 2560, 4096], P('grp', None, 'tp')
- grad_up: bfloat16 [8, 2560, 4096], P('grp', None, 'tp')
- grad_down: bfloat16 [8, 4096, 2560], P('grp', 'tp')
The draws below stay inside these ranges and needn't reach their ends.
Inputs may be any that keep to these rules, and one draw needn't show every extreme that they name: `expert_ids`: ids below 8 name the experts of this window; the others name experts outside it. A device routes at most 6 tokens to one expert of the window. `slots`: on one device, the tokens of one expert of the window hold the numbers 0 to n - 1, each once, where n is at least that expert's count; only those below the count are live. `counts`: at most the number of the device's tokens routed to that expert; in every draw some device has exactly 4 live rows for each expert of the window.
All inputs are finite; a program needn't handle non-finite values.
Results may differ from the reference program's by a relative error of at most 0.022.
Values may be sent and summed in bfloat16 or wider, within the bound.
A program may use at most 192 MiB of HBM per device.

```python
import math
import jax
import jax.numpy as jnp
from jax import lax

D = 2560
FF = 4096
FFS = 4096
EXP_ALL = 128
CAP = 4
TOK_DEV = 128
EXPERTS = 8
TOK_GRP = 2048
TOKENS = 16384
SOURCES = 128
ROWS = 512
FF_DEV = 256
SH_DEV = 256
N_GRP = 8
N_TP = 16


def route_tables(key):
    count_key, perm_key, other_key, slot_key, limit_key = jax.random.split(key, 5)
    drawn = jax.random.randint(count_key, (SOURCES, EXPERTS), 0, CAP + 3)
    limit = jax.random.randint(limit_key, (SOURCES, EXPERTS), 1, CAP + 1)
    source_iota = jnp.arange(SOURCES, dtype=jnp.int32)[:, None]
    expert_iota = jnp.arange(EXPERTS, dtype=jnp.int32)[None, :]
    full = source_iota % EXPERTS == expert_iota
    demand = jnp.where(full, CAP + 2, drawn).astype(jnp.int32)
    limit = jnp.where(full, CAP, limit).astype(jnp.int32)
    live_counts = jnp.minimum(demand, limit).astype(jnp.int32)
    ends = jnp.cumsum(demand, axis=1)
    begins = ends - demand
    place = jnp.arange(TOK_DEV, dtype=jnp.int32)[None, :, None]
    owner = jnp.sum((place >= ends[:, None, :]).astype(jnp.int32), axis=2)
    match = owner[:, :, None] == jnp.arange(EXPERTS, dtype=jnp.int32)[None, None, :]
    begin_of = jnp.sum(jnp.where(match, begins[:, None, :], 0), axis=2)
    inside = owner < EXPERTS
    other_ids = jax.random.randint(other_key, (SOURCES, TOK_DEV), EXPERTS, EXP_ALL)
    other_slots = jax.random.randint(slot_key, (SOURCES, TOK_DEV), 0, CAP)
    position = jnp.arange(TOK_DEV, dtype=jnp.int32)[None, :]
    id_table = jnp.where(inside, owner, other_ids).astype(jnp.int32)
    slot_table = jnp.where(inside, position - begin_of, other_slots).astype(jnp.int32)
    order = jax.vmap(lambda k: jax.random.permutation(k, TOK_DEV))(jax.random.split(perm_key, SOURCES))
    id_table = jnp.take_along_axis(id_table, order, axis=1)
    slot_table = jnp.take_along_axis(slot_table, order, axis=1)
    return (id_table.reshape(SOURCES * TOK_DEV), slot_table.reshape(SOURCES * TOK_DEV), live_counts)


def draw_expert_ids(key, part):
    return route_tables(key)[0]


def draw_slots(key, part):
    return route_tables(key)[1]


def draw_counts(key, part):
    return route_tables(key)[2]


def level_of(rng, shape, cuts, low, high):
    level, own = 1.0, jax.random.fold_in(rng, 6)
    for dim, blocks in cuts:
        heights = jnp.exp(jax.random.uniform(jax.random.fold_in(own, dim), (blocks,), jnp.float32, low / len(cuts), high / len(cuts)))
        level = level * jnp.repeat(heights, shape[dim] // blocks).reshape([-1 if axis == dim else 1 for axis in range(len(shape))])
    return level


def centred(rng, extent, deviation, reach, shards=(), kind=jnp.bfloat16):
    gain = level_of(rng, extent, shards, -0.22, 0.18) if shards else 1.0
    array = jax.random.normal(rng, extent, jnp.float32) * deviation * gain
    return jnp.minimum(jnp.maximum(array, -reach), reach).astype(kind)


def setup_inputs(seed: int = 0) -> dict:
    key_of = jax.random.split(jax.random.key(seed), 15)
    return {
        "tokens": centred(key_of[0], (TOKENS, D), 1.0, 6.0, ((0, 128),)),
        "grad_out": centred(key_of[1], (TOKENS, D), 1.0, 6.0, ((0, 128),)),
        "route_score": jnp.clip(jnp.exp(math.log(1.0) - 1.609438 * jax.random.uniform(key_of[2], (TOKENS,), jnp.float32) ** level_of(key_of[2], (TOKENS,), ((0, 128),), -0.2, 0.2)), 0.2, 1.0),
        "expert_ids": draw_expert_ids(jax.random.fold_in(key_of[14], 71), 0),
        "slots": draw_slots(jax.random.fold_in(key_of[14], 71), 0),
        "counts": draw_counts(jax.random.fold_in(key_of[14], 71), 0),
        "shared_gate_pre": centred(key_of[6], (TOKENS, FFS), 1.0, 6.0, ((0, 8), (1, 16))),
        "shared_up_pre": centred(key_of[7], (TOKENS, FFS), 1.0, 6.0, ((0, 8), (1, 16))),
        "shared_w_gate": centred(key_of[8], (D, FFS), D ** -0.5, 0.125, ((1, 16),)),
        "shared_w_up": centred(key_of[9], (D, FFS), D ** -0.5, 0.125, ((1, 16),)),
        "shared_w_down": centred(key_of[10], (FFS, D), FFS ** -0.5, 0.09375, ((0, 16),)),
        "w_gate": centred(key_of[11], (EXPERTS, D, FF), D ** -0.5, 0.125, ((0, 8), (2, 16))),
        "w_up": centred(key_of[12], (EXPERTS, D, FF), D ** -0.5, 0.125, ((0, 8), (2, 16))),
        "w_down": centred(key_of[13], (EXPERTS, FF, D), FF ** -0.5, 0.09375, ((0, 8), (1, 16))),
    }


def swish_parts(gate_pre, up_pre, hidden_grad):
    sigma = jax.nn.sigmoid(gate_pre)
    swish = gate_pre * sigma
    slope = sigma * (1.0 + gate_pre * (1.0 - sigma))
    return (hidden_grad * up_pre * slope).astype(jnp.bfloat16), (hidden_grad * swish).astype(jnp.bfloat16)


def contract_rows(left, right):
    return lax.dot_general(left, right, (((0,), (0,)), ((), ())), preferred_element_type=jnp.float32)


def contract_cols(left, right):
    return lax.dot_general(left, right, (((1,), (1,)), ((), ())), preferred_element_type=jnp.float32)


def reference(tokens, grad_out, route_score, expert_ids, slots, counts, shared_gate_pre, shared_up_pre, shared_w_gate, shared_w_up, shared_w_down, w_gate, w_up, w_down):
    gate_f = shared_gate_pre.astype(jnp.float32)
    up_f = shared_up_pre.astype(jnp.float32)
    shared_hidden = (jax.nn.silu(gate_f) * up_f).astype(jnp.bfloat16)
    shared_hgrad = contract_cols(grad_out, shared_w_down)
    shared_dgate, shared_dup = swish_parts(gate_f, up_f, shared_hgrad)

    def group_step(carry, start):
        rows_tok = lax.dynamic_slice_in_dim(tokens, start, TOK_GRP, 0)
        rows_grad = lax.dynamic_slice_in_dim(grad_out, start, TOK_GRP, 0)
        rows_hid = lax.dynamic_slice_in_dim(shared_hidden, start, TOK_GRP, 0)
        rows_gate = lax.dynamic_slice_in_dim(shared_dgate, start, TOK_GRP, 0)
        rows_up = lax.dynamic_slice_in_dim(shared_dup, start, TOK_GRP, 0)
        part_down = contract_rows(rows_hid, rows_grad).astype(jnp.bfloat16).astype(jnp.float32)
        part_gate = contract_rows(rows_tok, rows_gate).astype(jnp.bfloat16).astype(jnp.float32)
        part_up = contract_rows(rows_tok, rows_up).astype(jnp.bfloat16).astype(jnp.float32)
        return (carry[0] + part_gate, carry[1] + part_up, carry[2] + part_down), None

    starts = jnp.arange(N_GRP, dtype=jnp.int32) * TOK_GRP
    init = (jnp.zeros((D, FFS), jnp.float32), jnp.zeros((D, FFS), jnp.float32), jnp.zeros((FFS, D), jnp.float32))
    sums, _ = lax.scan(group_step, init, starts)
    grad_shared_gate = sums[0].astype(jnp.bfloat16)
    grad_shared_up = sums[1].astype(jnp.bfloat16)
    grad_shared_down = sums[2].astype(jnp.bfloat16)

    def block_step(carry, start):
        cols_gate = lax.dynamic_slice_in_dim(shared_dgate, start, SH_DEV, 1)
        cols_up = lax.dynamic_slice_in_dim(shared_dup, start, SH_DEV, 1)
        weight_gate = lax.dynamic_slice_in_dim(shared_w_gate, start, SH_DEV, 1)
        weight_up = lax.dynamic_slice_in_dim(shared_w_up, start, SH_DEV, 1)
        part = contract_cols(cols_gate, weight_gate) + contract_cols(cols_up, weight_up)
        return carry + part.astype(jnp.bfloat16).astype(jnp.float32), None

    block_starts = jnp.arange(N_TP, dtype=jnp.int32) * SH_DEV
    shared_grad_in, _ = lax.scan(block_step, jnp.zeros((TOKENS, D), jnp.float32), block_starts)

    source = jnp.arange(TOKENS, dtype=jnp.int32) // TOK_DEV
    safe_ids = jnp.clip(expert_ids, 0, EXPERTS - 1).astype(jnp.int32)
    own_count = counts[source, safe_ids]
    live = (expert_ids < EXPERTS) & (slots < own_count)
    row = safe_ids * ROWS + source * CAP + slots
    row = jnp.where(live, row, EXPERTS * ROWS).astype(jnp.int32)
    scaled = (route_score[:, None] * tokens.astype(jnp.float32)).astype(jnp.bfloat16)
    routed_in = jnp.zeros((EXPERTS * ROWS, D), jnp.float32).at[row].add(scaled.astype(jnp.float32), mode="drop")
    routed_in = routed_in.astype(jnp.bfloat16).reshape(EXPERTS, ROWS, D)
    routed_grad = jnp.zeros((EXPERTS * ROWS, D), jnp.float32).at[row].add(grad_out.astype(jnp.float32), mode="drop")
    routed_grad = routed_grad.astype(jnp.bfloat16).reshape(EXPERTS, ROWS, D)

    def one_expert(pack):
        rows_in, rows_grad, weight_gate, weight_up, weight_down = pack
        gate = jnp.dot(rows_in, weight_gate, preferred_element_type=jnp.float32)
        up = jnp.dot(rows_in, weight_up, preferred_element_type=jnp.float32)
        hidden = (jax.nn.silu(gate) * up).astype(jnp.bfloat16)
        hgrad = contract_cols(rows_grad, weight_down)
        dgate, dup = swish_parts(gate, up, hgrad)
        g_down = contract_rows(hidden, rows_grad).astype(jnp.bfloat16)
        g_gate = contract_rows(rows_in, dgate).astype(jnp.bfloat16)
        g_up = contract_rows(rows_in, dup).astype(jnp.bfloat16)

        def piece_step(carry, start):
            cols_gate = lax.dynamic_slice_in_dim(dgate, start, FF_DEV, 1)
            cols_up = lax.dynamic_slice_in_dim(dup, start, FF_DEV, 1)
            part_gate = lax.dynamic_slice_in_dim(weight_gate, start, FF_DEV, 1)
            part_up = lax.dynamic_slice_in_dim(weight_up, start, FF_DEV, 1)
            part = contract_cols(cols_gate, part_gate) + contract_cols(cols_up, part_up)
            return carry + part.astype(jnp.bfloat16).astype(jnp.float32), None

        piece_starts = jnp.arange(N_TP, dtype=jnp.int32) * FF_DEV
        back, _ = lax.scan(piece_step, jnp.zeros((ROWS, D), jnp.float32), piece_starts)
        return g_gate, g_up, g_down, back.astype(jnp.bfloat16)

    grad_gate, grad_up, grad_down, routed_back = lax.map(one_expert, (routed_in, routed_grad, w_gate, w_up, w_down))
    flat_back = routed_back.reshape(EXPERTS * ROWS, D)
    picked = flat_back[jnp.clip(row, 0, EXPERTS * ROWS - 1)].astype(jnp.float32)
    combined = jnp.where(live[:, None], picked, jnp.float32(0.0))
    grad_score = jnp.sum(tokens.astype(jnp.float32) * combined, axis=1)
    grad_tokens = (shared_grad_in + route_score[:, None] * combined).astype(jnp.bfloat16)
    return (grad_tokens, grad_score, grad_shared_gate, grad_shared_up, grad_shared_down, grad_gate, grad_up, grad_down)
```

```python
import functools

import jax
import jax.numpy as jnp
from jax import lax
from jax.experimental import pallas as pl
from jax.experimental.pallas import tpu as pltpu
from jax.sharding import PartitionSpec as P

CAP = 4
MESH = pl.DeviceIdType.MESH
BF, F32 = jnp.bfloat16, jnp.float32
ANY = pl.BlockSpec(memory_space=pl.ANY)
VM = pl.BlockSpec(memory_space=pltpu.VMEM)
SM = pl.BlockSpec(memory_space=pltpu.SMEM)
DIRS = (("+", 1), ("-", -1))


def dot_nn(a, b):
    return lax.dot_general(a, b, (((1,), (0,)), ((), ())), preferred_element_type=F32)


def dot_nt(a, b):
    return lax.dot_general(a, b, (((1,), (1,)), ((), ())), preferred_element_type=F32)


def dot_tn(a, b):
    return lax.dot_general(a, b, (((0,), (0,)), ((), ())), preferred_element_type=F32)


class Place:
    def __init__(self):
        self.g = lax.axis_index("grp")
        self.t = lax.axis_index("tp")
        self.xh, self.y = self.g // 4, self.g % 4
        self.xl, self.z, self.c = self.t // 8, (self.t // 2) % 4, self.t % 2

    def chip(self, dx, dz):
        return ((self.xl + dx) % 2) * 4 + (self.z + dz + 4) % 4

    def member(self, dx, dz, other=False):
        core = 1 - self.c if other else self.c
        return self.chip(dx, dz) * 2 + core

    def at(self, dx, dz, other=False):
        return (self.g, self.member(dx, dz, other))

    def group(self, dh, dy):
        return ((self.xh + dh) % 2) * 4 + (self.y + dy + 4) % 4

    def over(self, dh, dy):
        return (self.group(dh, dy), self.t)


def greet(targets):
    barrier = pltpu.get_barrier_semaphore()
    for target in targets:
        pl.semaphore_signal(barrier, inc=1, device_id=target, device_id_type=MESH)
    pl.semaphore_wait(barrier, len(targets))


def remote(src, dst, ss, rs, target):
    return pltpu.make_async_remote_copy(
        src_ref=src, dst_ref=dst, send_sem=ss, recv_sem=rs, device_id=target, device_id_type=MESH
    )


ARRIVE = {"xB": (1, 0, None, "B"), "xA0": (1, 0, None, "A")}
for _s, _d in DIRS:
    _h = 0 if _d > 0 else 1
    ARRIVE["zA" + _s] = (0, -_d, None, "A")
    ARRIVE["zB" + _s] = (0, -_d, None, "B")
    ARRIVE["zX" + _s] = (1, -_d, None, "B")
    ARRIVE["hA" + _s] = (0, 2, _h, "A")
    ARRIVE["hB" + _s] = (0, 2, _h, "B")
    ARRIVE["hX" + _s] = (1, 2, _h, "B")
    ARRIVE["xA" + _s] = (1, -_d, None, "A")
    ARRIVE["xh" + _s] = (1, 2, _h, "A")
SLOT = {name: i for i, name in enumerate(ARRIVE)}
N_ICI = len(SLOT)
N_SLOT = 2 * N_ICI + 1


class Gather:
    def __init__(self, place, buf, cut, ss, rs):
        self.p, self.buf, self.cut, self.ss, self.rs = place, buf, cut, ss, rs
        self.rows, self.width = buf.shape[1], buf.shape[2]
        self.sent = []

    def ref(self, member, half, part):
        rows = pl.ds(0, self.rows) if half is None else pl.ds(half * (self.rows // 2), self.rows // 2)
        cols = {
            None: pl.ds(0, self.width),
            "A": pl.ds(0, self.cut),
            "B": pl.ds(self.cut, self.width - self.cut),
        }[part]
        return self.buf.at[member, rows, cols]

    def send(self, slot, member, half, part, target):
        ref = self.ref(member, half, part)
        copy = remote(ref, ref, self.ss.at[slot], self.rs.at[slot], target)
        copy.start()
        self.sent.append(copy)

    def own(self):
        p, me = self.p, self.p.t
        for s, d in DIRS:
            self.send(SLOT["zA" + s], me, None, "A", p.at(0, d))
        self.send(SLOT["xB"], me, None, "B", p.at(1, 0))
        self.send(2 * N_ICI, me, None, None, p.at(0, 0, True))
        for s, d in DIRS:
            self.send(SLOT["zB" + s], me, None, "B", p.at(0, d))
        self.send(SLOT["xA0"], me, None, "A", p.at(1, 0))

    def take(self, *names):
        for name in names:
            self.take_one(name)

    def take_one(self, name):
        p = self.p
        dx, dz, half, part = ARRIVE[name]
        member = p.member(dx, dz)
        ref = self.ref(member, half, part)
        remote(ref, ref, self.ss.at[SLOT[name]], self.rs.at[SLOT[name]], p.at(1, 0)).wait_recv()
        kind, s = name[:2], name[2:]
        if name == "xB":
            for s2, d in DIRS:
                self.send(SLOT["zX" + s2], member, None, "B", p.at(0, d))
        if kind[0] == "z":
            d = 1 if s == "+" else -1
            if kind == "zA":
                self.send(SLOT["xA" + s], member, None, "A", p.at(1, 0))
            self.send(SLOT["h" + kind[1] + s], member, 0 if d > 0 else 1, part, p.at(0, d))
        if kind == "hA":
            self.send(SLOT["xh" + s], member, half, "A", p.at(1, 0))
        self.send(N_ICI + SLOT[name], member, half, part, p.at(0, 0, True))

    def twin(self, *names):
        for name in names:
            if name == "own":
                slot, ref = 2 * N_ICI, self.ref(self.p.member(0, 0, True), None, None)
            else:
                dx, dz, half, part = ARRIVE[name]
                slot, ref = N_ICI + SLOT[name], self.ref(self.p.member(dx, dz, True), half, part)
            remote(ref, ref, self.ss.at[slot], self.rs.at[slot], self.p.at(0, 0, True)).wait_recv()

    def finish(self):
        for copy in self.sent:
            copy.wait_send()


NEAR = ("own", "xB", "xA0", "zA+", "zA-", "zB+", "zB-")
MID = ("zX+", "zX-", "xA+", "xA-")
FAR = ("hA+", "hA-", "hB+", "hB-", "hX+", "hX-", "xh+", "xh-")


def positions(ids, slots, counts):
    own = jnp.zeros(ids.shape, jnp.int32)
    experts = counts.shape[1]
    for e in range(experts):
        own = own + jnp.where(ids == e, counts[0, e], 0)
    live = (ids < experts) & (slots < own)
    return jnp.where(live, ids * CAP + slots, -1)


def silu_parts(gate):
    sigma = jax.nn.sigmoid(gate)
    return gate * sigma, sigma * (1.0 + gate * (1.0 - sigma))


def forward_kernel(
    tok, grd, ids, slots, counts, score, gpre, upre, wds, wg, wu, wd,
    dgu, wpart, bk, ggate, gup, gdown,
    G, T, R, SB, RV, gp_v, up_v, wds_v, wg_v, wu_v, wd_v, dguT, hidT, acc_gu, acc_d,
    rgu, rguT, rhT, BP, BR, CS, MS, ggo, gdo,
    lsem, gss, grs, tss, trs, rss, rrs, ass, ars, bss, brs, dss, drs,
):
    p = Place()
    g, t, c = p.g, p.t, p.c
    peers = [((g + k) % 8, t) for k in range(1, 8)]
    loads = [
        pltpu.make_async_copy(grd, G.at[t], lsem.at[0]),
        pltpu.make_async_copy(tok, T.at[t], lsem.at[1]),
        pltpu.make_async_copy(wds, wds_v, lsem.at[2]),
        pltpu.make_async_copy(gpre, gp_v, lsem.at[3]),
        pltpu.make_async_copy(upre, up_v, lsem.at[4]),
        pltpu.make_async_copy(wg.at[0], wg_v, lsem.at[5]),
        pltpu.make_async_copy(wu.at[0], wu_v, lsem.at[6]),
        pltpu.make_async_copy(wd.at[0], wd_v, lsem.at[7]),
    ]
    for copy in loads:
        copy.start()
    greet([p.at(0, 1), p.at(0, -1), p.at(1, 0), p.at(0, 0, True)] + peers)
    gg = Gather(p, G, CUT, gss, grs)
    tg = Gather(p, T, CUT, tss, trs)
    rg = Gather(p, R, CUT, rss, rrs)
    loads[0].wait()
    gg.own()
    loads[1].wait()

    pos = positions(ids[...], slots[...], counts)
    n = SB.shape[0] * 16
    row = lax.broadcasted_iota(jnp.int32, (n, 128), 0)
    want = (row // 16) * CAP + row % CAP
    pick = pos == want
    scale = jnp.sum(jnp.where(pick, score[...], 0.0), axis=1, keepdims=True)
    pick = pick.astype(F32).astype(BF)
    wide = T.shape[2] // 2
    low = lax.broadcasted_iota(jnp.int32, (n, wide), 0) % 16 < 8
    grad = lax.broadcasted_iota(jnp.int32, (n, wide), 0) % 8 >= CAP
    vals_t = jnp.where(low, dot_nn(pick, T[t, :, 0:wide]), dot_nn(pick, T[t, :, wide:])) * scale
    vals_g = jnp.where(low, dot_nn(pick, G[t, :, 0:wide]), dot_nn(pick, G[t, :, wide:]))
    SB[...] = jnp.where(grad, vals_g, vals_t).astype(BF).reshape(SB.shape)
    sends = []
    for k in range(1, 8):
        e = (g + k) % 8
        copy = remote(SB.at[e], RV.at[g], ass.at[k], ars.at[k], (e, t))
        copy.start()
        sends.append(copy)
    RV[pl.ds(g, 1)] = SB[pl.ds(g, 1)]
    acc_d[...] = jnp.zeros_like(acc_d)
    acc_gu[...] = jnp.zeros_like(acc_gu)

    gg.take("xB", "zA+", "zA-")
    for k in range(1, 8):
        src = (g + 8 - k) % 8
        remote(SB.at[src], RV.at[src], ass.at[k], ars.at[k], (src, t)).wait_recv()
    rows = lax.broadcasted_iota(jnp.int32, (R.shape[1], n), 0)
    cols = lax.broadcasted_iota(jnp.int32, (R.shape[1], n), 1)
    base = ((rows % 32) // CAP) * 16 + (rows // 32) * CAP + rows % CAP
    got = RV[...].reshape(n, wide)
    R[t, :, 0:wide] = dot_nn((cols == base).astype(F32).astype(BF), got).astype(BF)
    R[t, :, wide:] = dot_nn((cols == base + 8).astype(F32).astype(BF), got).astype(BF)
    rg.own()
    gg.take("zB+", "zB-", "xA0", "zX+", "zX-")
    rg.take("xB", "zA+", "zA-")
    gg.take("hA+", "hA-", "xA+", "xA-")
    tg.own()
    rg.take("zB+", "zB-", "xA0", "zX+", "zX-")
    gg.take("hB+", "hB-", "hX+", "hX-", "xh+", "xh-")
    rg.take("hA+", "hA-", "xA+", "xA-")
    tg.take("xB")
    gg.twin(*NEAR, *MID, *FAR)
    for copy in loads[2:5]:
        copy.wait()

    def g_unit(j, carry):
        two = pl.ds(2 * j, 2)
        toks = pl.ds(pl.multiple_of(j * 256, 256), 256)
        h = dot_nt(G[two].reshape(256, G.shape[2]), wds_v[...])
        gate, up = gp_v[toks].astype(F32), up_v[toks].astype(F32)
        silu, slope = silu_parts(gate)
        dg, du = h * up * slope, h * silu
        dgu[two, :, 0:256] = dg.astype(BF).reshape(2, 128, 256)
        dgu[two, :, 256:512] = du.astype(BF).reshape(2, 128, 256)
        dguT[j, 0:256] = dg.T.astype(BF)
        dguT[j, 256:512] = du.T.astype(BF)
        hidT[...] = (silu * up).T.astype(BF)

        def part(i, carry):
            cs = pl.ds(pl.multiple_of(i * 512, 512), 512)
            acc_d[:, cs] += dot_nn(hidT[...], G[two, :, cs].reshape(256, 512))
            return carry

        return lax.fori_loop(0, G.shape[2] // 512, part, carry)

    def t_unit(j):
        two = pl.ds(2 * j, 2)

        def part(i, carry):
            cs = pl.ds(pl.multiple_of(i * 512, 512), 512)
            acc_gu[:, cs] += dot_nn(dguT[j], T[two, :, cs].reshape(256, 512))
            return carry

        lax.fori_loop(0, T.shape[2] // 512, part, 0)

    lax.fori_loop(0, 3, g_unit, 0)
    rg.take("hB+", "hB-", "hX+", "hX-", "xh+", "xh-")
    tg.take("zA+", "zA-")
    lax.fori_loop(3, 8, g_unit, 0)
    rg.twin(*NEAR, *MID, *FAR)
    tg.take("zB+", "zB-")
    for copy in loads[5:8]:
        copy.wait()

    def r_unit(m, carry):
        mem = pl.ds(8 * m, 8)
        rin = R[mem, 0:32].reshape(256, R.shape[2])
        rgr = R[mem, 32:64].reshape(256, R.shape[2])
        gate, up = dot_nn(rin, wg_v[...]), dot_nn(rin, wu_v[...])
        h = dot_nt(rgr, wd_v[...])
        silu, slope = silu_parts(gate)
        dg, du = h * up * slope, h * silu
        dgb, dub = dg.astype(BF), du.astype(BF)
        at = pl.ds(pl.multiple_of(m * 256, 256), 256)
        rgu[at, 0:256] = dgb
        rgu[at, 256:512] = dub
        rguT[0:256, at] = dg.T.astype(BF)
        rguT[256:512, at] = du.T.astype(BF)
        rhT[:, at] = (silu * up).T.astype(BF)
        q = jnp.sum(dgb.astype(F32) * gate + dub.astype(F32) * up, axis=1, keepdims=True)
        hi = q.astype(BF).astype(F32)
        lane = lax.broadcasted_iota(jnp.int32, (256, 128), 1)
        tail = jnp.where(lane == 0, hi, jnp.where(lane == 1, q - hi, 0.0)).astype(BF)
        BP[pl.ds(4 * m, 4), :, :, R.shape[2] :] = tail.reshape(4, 2, 32, 128)
        return carry

    lax.fori_loop(0, 2, r_unit, 0)

    def b_unit(i, carry):
        cs = pl.ds(pl.multiple_of(i * 512, 512), 512)
        out = dot_nt(rgu[:, 0:256], wg_v[cs]) + dot_nt(rgu[:, 256:512], wu_v[cs])
        BP[:, :, :, cs] = out.astype(BF).reshape(8, 2, 32, 512)
        return carry

    lax.fori_loop(0, R.shape[2] // 512, b_unit, 0)
    across = remote(BP.at[:, 1 - c], BR, dss.at[0], drs.at[0], p.at(0, 0, True))
    across.start()
    tg.take("xA0", "zX+", "zX-")

    def w_unit(i, carry):
        cs = pl.ds(pl.multiple_of(i * 256, 256), 256)
        rin = R[:, 0:32, cs].reshape(512, 256)
        rgr = R[:, 32:64, cs].reshape(512, 256)
        gu = dot_nn(rguT[...], rin)
        ggo[0, cs] = gu[0:256].T.astype(BF)
        ggo[1, cs] = gu[256:512].T.astype(BF)
        gdo[:, cs] = dot_nn(rhT[...], rgr).astype(BF)
        return carry

    remote(BP.at[:, c], BR, dss.at[0], drs.at[0], p.at(0, 0, True)).wait_recv()

    def s_unit(i, carry):
        CS[pl.ds(i, 1)] = (BP[pl.ds(i, 1), c].astype(F32) + BR[pl.ds(i, 1)].astype(F32)).astype(BF)
        return carry

    lax.fori_loop(0, 8, s_unit, 0)
    r0 = lax.broadcasted_iota(jnp.int32, (256, 256), 0)
    r1 = lax.broadcasted_iota(jnp.int32, (256, 256), 1)
    turn = (r1 == ((r0 // CAP) % 8) * 32 + (r0 // 32) * CAP + r0 % CAP).astype(F32).astype(BF)
    MS[...] = dot_nn(turn, CS[...].reshape(256, CS.shape[2])).astype(BF).reshape(MS.shape)
    for k in range(1, 8):
        e = (g + k) % 8
        copy = remote(MS.at[e], bk.at[g], bss.at[k], brs.at[k], (e, t))
        copy.start()
        sends.append(copy)
    keep = pltpu.make_async_copy(MS.at[g], bk.at[g], lsem.at[8])
    keep.start()
    tg.take("hA+", "hA-", "xA+", "xA-")
    lax.fori_loop(0, R.shape[2] // 256, w_unit, 0)
    outs = [
        pltpu.make_async_copy(ggo.at[0], ggate.at[0], lsem.at[9]),
        pltpu.make_async_copy(ggo.at[1], gup.at[0], lsem.at[10]),
        pltpu.make_async_copy(gdo, gdown.at[0], lsem.at[11]),
    ]
    for copy in outs:
        copy.start()
    tg.twin(*NEAR)
    t_unit(p.chip(0, 0))
    t_unit(p.chip(1, 0))
    t_unit(p.chip(0, 1))
    t_unit(p.chip(0, -1))
    tg.take("hB+", "hB-", "hX+", "hX-", "xh+", "xh-")
    tg.twin(*MID)
    t_unit(p.chip(1, 1))
    t_unit(p.chip(1, -1))
    tg.twin(*FAR)
    t_unit(p.chip(0, 2))
    t_unit(p.chip(1, 2))

    def turn_unit(i, carry):
        cs = pl.ds(pl.multiple_of(i * 256, 256), 256)
        wpart[0, cs] = acc_gu[0:256, cs].T.astype(BF)
        wpart[1, cs] = acc_gu[256:512, cs].T.astype(BF)
        wpart[2, cs] = acc_d[:, cs].T.astype(BF)
        return carry

    lax.fori_loop(0, T.shape[2] // 256, turn_unit, 0)
    keep.wait()
    for copy in outs:
        copy.wait()
    for k in range(1, 8):
        src = (g + 8 - k) % 8
        remote(MS.at[src], bk.at[src], bss.at[k], brs.at[k], (src, t)).wait_recv()
    across.wait_send()
    for copy in sends:
        copy.wait_send()
    gg.finish()
    tg.finish()
    rg.finish()


CUT = 1152
RCUT = 768


def reduce_kernel(
    dgu, wgs, wus, bk, wpart, ids, slots, counts, score,
    gtok, gscore, gw,
    S, DS, DR, XA, ZH, ZF, XB, W, WH, WF, WX, info, mine, QS, QR,
    lsem, dss, drs, xss, xrs, zss, zrs, wss, wrs, iss, irs, qss, qrs,
):
    p = Place()
    c = p.c
    width = gtok.shape[1]
    load = pltpu.make_async_copy(wpart, W, lsem.at[0])
    load.start()
    chips = [(dx, dz) for dx in range(2) for dz in range(4) if (dx, dz) != (0, 0)]
    greet(
        [p.at(dx, dz) for dx, dz in chips]
        + [p.at(0, 0, True), p.over(0, 1), p.over(0, -1), p.over(1, 0)]
    )
    sends = []

    def ship(src, dst, ss, rs, target):
        copy = remote(src, dst, ss, rs, target)
        copy.start()
        sends.append(copy)

    def land(ref, ss, rs):
        remote(ref, ref, ss, rs, p.at(0, 0, True)).wait_recv()

    pos = positions(ids[...], slots[...], counts)
    which = lax.broadcasted_iota(jnp.int32, (8, 128), 0)
    mine[...] = jnp.where(which == 0, pos.astype(F32), score[...])
    for i, (dx, dz) in enumerate(chips):
        ship(mine, info.at[dx, (4 - dz) % 4], iss.at[i], irs.at[i], p.at(dx, dz))
    info[0, 0] = mine[...]

    load.wait()
    half = (pl.ds(0, 160), pl.ds(160, 160))
    for dh in range(2):
        for i, (s, d) in enumerate(DIRS):
            ship(W.at[:, p.group(dh, 2), half[i]], WH.at[dh, i], wss.at[dh, i], wrs.at[dh, i], p.over(0, d))

    def weights_second():
        for dh in (1, 0):
            for i, (s, d) in enumerate(DIRS):
                land(WH.at[dh, i], wss.at[dh, i], wrs.at[dh, i])
                at = p.group(dh, d)
                for a in range(3):
                    W[a, at, half[i]] = (W[a, at, half[i]].astype(F32) + WH[dh, i, a].astype(F32)).astype(BF)
                ship(W.at[:, at], WF.at[dh, i], wss.at[dh, 2 + i], wrs.at[dh, 2 + i], p.over(0, d))

    def weights_third():
        for i in range(2):
            land(WF.at[1, i], wss.at[1, 2 + i], wrs.at[1, 2 + i])
        at = p.group(1, 0)
        for a in range(3):
            total = W[a, at].astype(F32) + WF[1, 0, a].astype(F32) + WF[1, 1, a].astype(F32)
            W[a, at] = total.astype(BF)
        ship(W.at[:, at], WX, wss.at[0, 4], wrs.at[0, 4], p.over(1, 0))

    def weights_last():
        for i in range(2):
            land(WF.at[0, i], wss.at[0, 2 + i], wrs.at[0, 2 + i])
        land(WX, wss.at[0, 4], wrs.at[0, 4])
        at = p.group(0, 0)
        for a in range(3):
            total = W[a, at].astype(F32) + WF[0, 0, a].astype(F32) + WF[0, 1, a].astype(F32) + WX[a].astype(F32)
            gw[a] = total.astype(BF)

    def make(dx, dz):
        j = p.chip(dx, dz)
        slot = dx * 4 + dz

        def part(i, carry):
            cs = pl.ds(pl.multiple_of(i * 512, 512), 512)
            two = dgu[pl.ds(2 * j, 2)].reshape(256, 512)
            out = dot_nt(two[:, 0:256], wgs[cs]) + dot_nt(two[:, 256:512], wus[cs])
            DS[slot, :, :, cs] = out.astype(BF).reshape(2, 128, 512)
            return carry

        lax.fori_loop(0, width // 512, part, 0)
        ship(DS.at[slot, 1 - c], DR.at[slot], dss.at[slot], drs.at[slot], p.at(0, 0, True))

    row = lax.broadcasted_iota(jnp.int32, (256, 128), 0)
    want = ((row // 32) * CAP + row % CAP).astype(F32)

    def join(dx, dz, first):
        j = p.chip(dx, dz)
        slot = dx * 4 + dz
        if (dx, dz) != (0, 0):
            i = chips.index((dx, (4 - dz) % 4))
            land(info.at[dx, dz], iss.at[i], irs.at[i])
        pick = (want == info[dx, dz, 0:1]) & ((row // CAP) % 8 == j)
        scale = jnp.sum(jnp.where(pick, info[dx, dz, 1:2], 0.0), axis=1, keepdims=True)
        pickT = pick.astype(F32).T.astype(BF)
        pick = pick.astype(F32).astype(BF)
        q = dot_tn(bk[:, :, width:].reshape(256, 128), pick)
        QS[dx, dz] = jnp.broadcast_to(q[0:1] + q[1:2], (8, 128))
        land(DR.at[slot], dss.at[slot], drs.at[slot])

        def part(i, carry):
            cs = pl.ds(pl.multiple_of(i * 512, 512), 512)
            rows = (bk[:, :, cs].reshape(256, 512).astype(F32) * scale).astype(BF)
            total = dot_nn(pickT, rows) + DS[slot, c, :, cs].astype(F32) + DR[slot, :, cs].astype(F32)
            S[slot, :, cs] = total.astype(BF)
            return carry

        lax.fori_loop(0, width // 512, part, 0)
        if (dx, dz) != (0, 0):
            i = chips.index((dx, dz))
            ship(QS.at[dx, dz], QR.at[i], qss.at[i], qrs.at[i], p.at(dx, dz))

    colA, colB = pl.ds(0, RCUT), pl.ds(RCUT, width - RCUT)
    rowh = (pl.ds(0, 64), pl.ds(64, 64))

    def cols_of(lane):
        return colA if lane == 2 else colB

    def box(ref, lane, *idx):
        return ref.at[(lane,) + idx + (pl.ds(0, RCUT if lane == 2 else width - RCUT),)]

    def z_first(lane):
        slot = (lane % 2) * 4 + 2
        for i, (s, d) in enumerate(DIRS):
            ship(S.at[slot, rowh[i], cols_of(lane)], box(ZH, lane, i, pl.ds(0, 64)), zss.at[lane, i], zrs.at[lane, i], p.at(0, d))

    def z_second(lane):
        for i, (s, d) in enumerate(DIRS):
            slot = (lane % 2) * 4 + d % 4
            ref = box(ZH, lane, i, pl.ds(0, 64))
            land(ref, zss.at[lane, i], zrs.at[lane, i])
            S[slot, rowh[i], cols_of(lane)] = (
                S[slot, rowh[i], cols_of(lane)].astype(F32) + ref[...].astype(F32)
            ).astype(BF)
            ship(S.at[slot, :, cols_of(lane)], box(ZF, lane, i, pl.ds(0, 128)), zss.at[lane, 2 + i], zrs.at[lane, 2 + i], p.at(0, d))

    def z_third(lane):
        for i in range(2):
            land(box(ZF, lane, i, pl.ds(0, 128)), zss.at[lane, 2 + i], zrs.at[lane, 2 + i])
        slot = (lane % 2) * 4
        return (
            S[slot, :, cols_of(lane)].astype(F32)
            + box(ZF, lane, 0, pl.ds(0, 128))[...].astype(F32)
            + box(ZF, lane, 1, pl.ds(0, 128))[...].astype(F32)
        )

    def x_send(dz):
        ship(S.at[4 + dz, :, colA], XA.at[dz], xss.at[dz], xrs.at[dz], p.at(1, 0))

    def x_add(dz):
        land(XA.at[dz], xss.at[dz], xrs.at[dz])
        S[dz, :, colA] = (S[dz, :, colA].astype(F32) + XA[dz].astype(F32)).astype(BF)

    make(1, 2)
    make(0, 2)
    join(1, 2, True)
    x_send(2)
    z_first(1)
    make(1, 1)
    join(0, 2, True)
    z_first(0)
    make(1, 3)
    join(1, 1, True)
    x_send(1)
    make(0, 1)
    join(1, 3, True)
    x_send(3)
    x_add(2)
    z_first(2)
    make(0, 3)
    z_second(1)
    join(0, 1, True)
    make(1, 0)
    join(0, 3, True)
    z_second(0)
    weights_second()
    join(1, 0, True)
    x_send(0)
    make(0, 0)
    x_add(1)
    x_add(3)
    z_second(2)
    join(0, 0, True)
    S[4, :, colB] = z_third(1).astype(BF)
    ship(S.at[4, :, colB], XB, xss.at[4], xrs.at[4], p.at(1, 0))
    weights_third()
    partB = z_third(0)
    land(XB, xss.at[4], xrs.at[4])
    gtok[:, colB] = (partB + XB[...].astype(F32)).astype(BF)
    x_add_last = XA.at[0]
    land(x_add_last, xss.at[0], xrs.at[0])
    gtok[:, colA] = (z_third(2) + XA[0].astype(F32)).astype(BF)
    total = QS[0, 0]
    for i, (dx, dz) in enumerate(chips):
        land(QR.at[i], qss.at[i], qrs.at[i])
        total = total + QR[i]
    gscore[...] = total / score[...]
    weights_last()
    for copy in sends:
        copy.wait_send()


def shards(
    tokens, grad_out, route_score, expert_ids, slots, counts, shared_gate_pre, shared_up_pre,
    shared_w_gate, shared_w_up, shared_w_down, w_gate, w_up, w_down,
):
    tok_dev, width = tokens.shape
    ff = w_gate.shape[2]
    ids, slt, score = (a.reshape(1, tok_dev) for a in (expert_ids, slots, route_score))
    dma = pltpu.SemaphoreType.DMA
    wide = width + 128
    dgu, wpart, bk, ggate, gup, gdown = pl.pallas_call(
        forward_kernel,
        out_shape=(
            jax.ShapeDtypeStruct((16, tok_dev, 2 * ff), BF),
            jax.ShapeDtypeStruct((3, width, ff), BF),
            jax.ShapeDtypeStruct((8, 32, wide), BF),
            jax.ShapeDtypeStruct((1, width, ff), BF),
            jax.ShapeDtypeStruct((1, width, ff), BF),
            jax.ShapeDtypeStruct((1, ff, width), BF),
        ),
        in_specs=[ANY, ANY, VM, VM, SM, VM, ANY, ANY, ANY, ANY, ANY, ANY],
        out_specs=(VM, VM, ANY, ANY, ANY, ANY),
        scratch_shapes=[
            pltpu.VMEM((16, tok_dev, width), BF),
            pltpu.VMEM((16, tok_dev, width), BF),
            pltpu.VMEM((16, 64, width), BF),
            pltpu.VMEM((8, 16, width // 2), BF),
            pltpu.VMEM((8, 16, width // 2), BF),
            pltpu.VMEM((16 * tok_dev, ff), BF),
            pltpu.VMEM((16 * tok_dev, ff), BF),
            pltpu.VMEM((ff, width), BF),
            pltpu.VMEM((width, ff), BF),
            pltpu.VMEM((width, ff), BF),
            pltpu.VMEM((ff, width), BF),
            pltpu.VMEM((8, 2 * ff, 256), BF),
            pltpu.VMEM((ff, 256), BF),
            pltpu.VMEM((2 * ff, width), F32),
            pltpu.VMEM((ff, width), F32),
            pltpu.VMEM((512, 2 * ff), BF),
            pltpu.VMEM((2 * ff, 512), BF),
            pltpu.VMEM((ff, 512), BF),
            pltpu.VMEM((8, 2, 32, wide), BF),
            pltpu.VMEM((8, 32, wide), BF),
            pltpu.VMEM((8, 32, wide), BF),
            pltpu.VMEM((8, 32, wide), BF),
            pltpu.VMEM((2, width, ff), BF),
            pltpu.VMEM((ff, width), BF),
            dma((12,)),
            dma((N_SLOT,)), dma((N_SLOT,)),
            dma((N_SLOT,)), dma((N_SLOT,)),
            dma((N_SLOT,)), dma((N_SLOT,)),
            dma((8,)), dma((8,)),
            dma((8,)), dma((8,)),
            dma((1,)), dma((1,)),
        ],
        compiler_params=pltpu.CompilerParams(
            collective_id=0, has_side_effects=True, vmem_limit_bytes=63 << 20
        ),
    )(
        tokens, grad_out, ids, slt, counts, score, shared_gate_pre, shared_up_pre,
        shared_w_down, w_gate, w_up, w_down,
    )
    gtok, gscore, gw = pl.pallas_call(
        reduce_kernel,
        out_shape=(
            jax.ShapeDtypeStruct((tok_dev, width), BF),
            jax.ShapeDtypeStruct((8, tok_dev), F32),
            jax.ShapeDtypeStruct((3, width // 8, ff), BF),
        ),
        in_specs=[VM, VM, VM, VM, ANY, VM, VM, SM, VM],
        out_specs=(VM, VM, VM),
        scratch_shapes=[
            pltpu.VMEM((8, tok_dev, width), BF),
            pltpu.VMEM((8, 2, tok_dev, width), BF),
            pltpu.VMEM((8, tok_dev, width), BF),
            pltpu.VMEM((4, tok_dev, RCUT), BF),
            pltpu.VMEM((3, 2, 64, width - RCUT), BF),
            pltpu.VMEM((3, 2, tok_dev, width - RCUT), BF),
            pltpu.VMEM((tok_dev, width - RCUT), BF),
            pltpu.VMEM((3, 8, width // 8, ff), BF),
            pltpu.VMEM((2, 2, 3, width // 16, ff), BF),
            pltpu.VMEM((2, 2, 3, width // 8, ff), BF),
            pltpu.VMEM((3, width // 8, ff), BF),
            pltpu.VMEM((2, 4, 8, 128), F32),
            pltpu.VMEM((8, 128), F32),
            pltpu.VMEM((2, 4, 8, 128), F32),
            pltpu.VMEM((7, 8, 128), F32),
            dma((1,)),
            dma((8,)), dma((8,)),
            dma((5,)), dma((5,)),
            dma((3, 4)), dma((3, 4)),
            dma((2, 5)), dma((2, 5)),
            dma((7,)), dma((7,)),
            dma((7,)), dma((7,)),
        ],
        compiler_params=pltpu.CompilerParams(
            collective_id=1, has_side_effects=True, vmem_limit_bytes=63 << 20
        ),
    )(
        dgu, shared_w_gate, shared_w_up, bk, wpart.reshape(3, 8, width // 8, ff), ids, slt, counts, score,
    )
    return (gtok, gscore[0], gw[0], gw[1], gw[2].T, ggate, gup, gdown)


def solution(mesh):
    placed = (
        P(("grp", "tp"), None),
        P(("grp", "tp"), None),
        P(("grp", "tp")),
        P(("grp", "tp")),
        P(("grp", "tp")),
        P(("grp", "tp"), None),
        P("grp", "tp"),
        P("grp", "tp"),
        P(None, "tp"),
        P(None, "tp"),
        P("tp", None),
        P("grp", None, "tp"),
        P("grp", None, "tp"),
        P("grp", "tp", None),
    )
    return jax.shard_map(
        shards,
        mesh=mesh,
        in_specs=placed,
        out_specs=(
            P(("grp", "tp"), None),
            P(("grp", "tp")),
            P("grp", "tp"),
            P("grp", "tp"),
            P("tp", "grp"),
            P("grp", None, "tp"),
            P("grp", None, "tp"),
            P("grp", "tp", None),
        ),
        check_vma=False,
    )
```

```python
import functools

import jax
import jax.numpy as jnp
from jax import lax
from jax.experimental import pallas as pl
from jax.experimental.pallas import tpu as pltpu
from jax.sharding import PartitionSpec as P

CAP = 4
MESH = pl.DeviceIdType.MESH
BF, F32 = jnp.bfloat16, jnp.float32
ANY = pl.BlockSpec(memory_space=pl.ANY)
VM = pl.BlockSpec(memory_space=pltpu.VMEM)
SM = pl.BlockSpec(memory_space=pltpu.SMEM)
DIRS = (("+", 1), ("-", -1))


def dot_nn(a, b):
    return lax.dot_general(a, b, (((1,), (0,)), ((), ())), preferred_element_type=F32)


def dot_nt(a, b):
    return lax.dot_general(a, b, (((1,), (1,)), ((), ())), preferred_element_type=F32)


def dot_tn(a, b):
    return lax.dot_general(a, b, (((0,), (0,)), ((), ())), preferred_element_type=F32)


class Place:
    def __init__(self):
        self.g = lax.axis_index("grp")
        self.t = lax.axis_index("tp")
        self.xh, self.y = self.g // 4, self.g % 4
        self.xl, self.z, self.c = self.t // 8, (self.t // 2) % 4, self.t % 2

    def chip(self, dx, dz):
        return ((self.xl + dx) % 2) * 4 + (self.z + dz + 4) % 4

    def member(self, dx, dz, other=False):
        core = 1 - self.c if other else self.c
        return self.chip(dx, dz) * 2 + core

    def at(self, dx, dz, other=False):
        return (self.g, self.member(dx, dz, other))

    def group(self, dh, dy):
        return ((self.xh + dh) % 2) * 4 + (self.y + dy + 4) % 4

    def over(self, dh, dy):
        return (self.group(dh, dy), self.t)

    def peer(self, dh, dy):
        return (self.group(dh, dy), (self.t + 8 * dh) % 16)


def greet(targets):
    barrier = pltpu.get_barrier_semaphore()
    for target in targets:
        pl.semaphore_signal(barrier, inc=1, device_id=target, device_id_type=MESH)
    pl.semaphore_wait(barrier, len(targets))


def remote(src, dst, ss, rs, target):
    return pltpu.make_async_remote_copy(
        src_ref=src, dst_ref=dst, send_sem=ss, recv_sem=rs, device_id=target, device_id_type=MESH
    )


ARRIVE = {"xB": (1, 0, None, "B"), "xA0": (1, 0, None, "A")}
for _s, _d in DIRS:
    _h = 0 if _d > 0 else 1
    ARRIVE["zA" + _s] = (0, -_d, None, "A")
    ARRIVE["zB" + _s] = (0, -_d, None, "B")
    ARRIVE["zX" + _s] = (1, -_d, None, "B")
    ARRIVE["hA" + _s] = (0, 2, _h, "A")
    ARRIVE["hB" + _s] = (0, 2, _h, "B")
    ARRIVE["hX" + _s] = (1, 2, _h, "B")
    ARRIVE["xA" + _s] = (1, -_d, None, "A")
    ARRIVE["xh" + _s] = (1, 2, _h, "A")
SLOT = {name: i for i, name in enumerate(ARRIVE)}
N_ICI = len(SLOT)
N_SLOT = 2 * N_ICI + 1


class Gather:
    def __init__(self, place, buf, cut, ss, rs):
        self.p, self.buf, self.cut, self.ss, self.rs = place, buf, cut, ss, rs
        self.rows, self.width = buf.shape[1], buf.shape[2]
        self.sent = {}

    def ref(self, member, half, part):
        rows = pl.ds(0, self.rows) if half is None else pl.ds(half * (self.rows // 2), self.rows // 2)
        cols = {
            None: pl.ds(0, self.width),
            "A": pl.ds(0, self.cut),
            "B": pl.ds(self.cut, self.width - self.cut),
        }[part]
        return self.buf.at[member, rows, cols]

    def send(self, slot, chip, half, part, target):
        ref = self.ref(self.p.member(*chip), half, part)
        copy = remote(ref, ref, self.ss.at[slot], self.rs.at[slot], target)
        copy.start()
        self.sent.setdefault((chip[0], chip[1] % 4), []).append(copy)

    def own(self):
        p, me = self.p, (0, 0)
        for s, d in DIRS:
            self.send(SLOT["zA" + s], me, None, "A", p.at(0, d))
        self.send(SLOT["xB"], me, None, "B", p.at(1, 0))
        self.send(2 * N_ICI, me, None, None, p.at(0, 0, True))

    def own_rest(self):
        p, me = self.p, (0, 0)
        for s, d in DIRS:
            self.send(SLOT["zB" + s], me, None, "B", p.at(0, d))
        self.send(SLOT["xA0"], me, None, "A", p.at(1, 0))

    def take(self, *names):
        for name in names:
            self.take_one(name)

    def take_one(self, name):
        p = self.p
        dx, dz, half, part = ARRIVE[name]
        member = (dx, dz)
        ref = self.ref(p.member(dx, dz), half, part)
        remote(ref, ref, self.ss.at[SLOT[name]], self.rs.at[SLOT[name]], p.at(1, 0)).wait_recv()
        kind, s = name[:2], name[2:]
        if name == "xB":
            for s2, d in DIRS:
                self.send(SLOT["zX" + s2], member, None, "B", p.at(0, d))
        if kind[0] == "z":
            d = 1 if s == "+" else -1
            if kind == "zA":
                self.send(SLOT["xA" + s], member, None, "A", p.at(1, 0))
            self.send(SLOT["h" + kind[1] + s], member, 0 if d > 0 else 1, part, p.at(0, d))
        if kind == "hA":
            self.send(SLOT["xh" + s], member, half, "A", p.at(1, 0))
        self.send(N_ICI + SLOT[name], member, half, part, p.at(0, 0, True))

    def twin(self, *names):
        for name in names:
            if name == "own":
                slot, ref = 2 * N_ICI, self.ref(self.p.member(0, 0, True), None, None)
            else:
                dx, dz, half, part = ARRIVE[name]
                slot, ref = N_ICI + SLOT[name], self.ref(self.p.member(dx, dz, True), half, part)
            remote(ref, ref, self.ss.at[slot], self.rs.at[slot], self.p.at(0, 0, True)).wait_recv()

    def finish(self, chip=None):
        for key in list(self.sent) if chip is None else [(chip[0], chip[1] % 4)]:
            for copy in self.sent.pop(key, []):
                copy.wait_send()


CHIP = ((0, 0), (1, 0), (0, -1), (0, 1), (1, -1), (1, 1), (0, 2), (1, 2))
NEED = (
    ("own",),
    ("xB", "xA0"),
    ("zA+", "zB+"),
    ("zA-", "zB-"),
    ("zX+", "xA+"),
    ("zX-", "xA-"),
    ("hA+", "hA-", "hB+", "hB-"),
    ("hX+", "hX-", "xh+", "xh-"),
)
PEERS = [(dh, dy) for dh in range(2) for dy in range(4) if (dh, dy) != (0, 0)]
MATES = [(dx, dz) for dx in range(2) for dz in range(4) if (dx, dz) != (0, 0)]
CUT = 1152
RCUT = 1024
ORDER = (
    "G0", "g2", "Rown", "r2", "rzA+", "rzA-", "rxB", "M00", "rzB-", "rzB+", "rhA+", "rhA-", "rxA0",
    "rzX+", "rzX-", "rhB+", "rhB-", "rxA+", "rxA-", "rxh+", "gzA+", "gzA-", "gxB", "gzB+", "gzB-",
    "gxA0", "rxh-", "rhX+", "rhX-", "R0", "Town", "R1", "Rb", "L0", "G1", "ghA+", "ghA-", "t2", "G2",
    "T0", "ghB+", "Rs", "ghB-", "G3", "Rw0", "gxA+", "gxA-", "G6", "Rw1", "Rf", "M01", "gzX+", "gzX-",
    "tzA+", "tzA-", "M03", "gxh+", "gxh-", "N01", "N03", "N00", "M02", "N02", "G4", "tzB+", "tzB-",
    "G5", "M10", "N10", "J01", "J03", "thA+", "txB", "thA-", "ghX+", "ghX-", "J02", "J00", "txA0",
    "J10", "L2", "thB+", "L3", "M11", "thB-", "N11", "G7", "T2", "T3", "J11", "Z10", "S1", "S0", "L1",
    "tzX+", "L6", "tzX-", "D0", "M12", "N12", "M13", "N13", "T1", "txh+", "txA+", "T6", "txA-", "txh-",
    "J12", "Z11", "S2", "J13", "S3", "L4", "D1", "thX+", "thX-", "Z20", "L5", "T4", "L7", "T5", "Z21",
    "T7", "W0", "D2", "X1", "W0b", "W11", "W10", "X2", "Z12", "X3", "D3", "Z31", "Z22", "W2", "F0",
    "F2", "W3",
)


def positions(ids, slots, counts):
    own = jnp.zeros(ids.shape, jnp.int32)
    experts = counts.shape[1]
    for e in range(experts):
        own = own + jnp.where(ids == e, counts[0, e], 0)
    live = (ids < experts) & (slots < own)
    return jnp.where(live, ids * CAP + slots, -1)


def silu_parts(gate):
    sigma = jax.nn.sigmoid(gate)
    return gate * sigma, sigma * (1.0 + gate * (1.0 - sigma))


def kernel(
    tok, grd, ids, slots, counts, score, gpre, upre, wds, wgs, wus, wg, wu, wd,
    gtok, gscore, gsg, gsd, ggate, gup, gdown, TH,
    G, R, TV, SB, RV, dg_v, du_v, wds_v, wgs_v, wus_v, wg_v, wu_v, wd_v, dguT, hidT, acc_gu, acc_d,
    rgu, rguT, rhT, BP, BR, MS, BK, WS, W, WH, WF, WX, WD, DH, DF, DX,
    XA, ZH, ZF, XB, info, mine, QS, QR,
    lsem, tsem, wsem, gss, grs, tss, trs, rss, rrs, ass, ars, bss, brs, dss, drs, css, crs,
    xss, xrs, zss, zrs, wss, wrs, hss, hrs, iss, irs, qss, qrs, credit,
):
    p = Place()
    g, t, c = p.g, p.t, p.c
    width = gtok.shape[1]
    pieces = ((grd, G.at[t]), (tok, TV.at[0, 0]), (TV.at[0, 0], TH.at[t]), (wds, wds_v), (gpre, dg_v), (upre, du_v),
              (wg.at[0], wg_v), (wu.at[0], wu_v), (wd.at[0], wd_v), (wgs, wgs_v), (wus, wus_v))
    loads = [pltpu.make_async_copy(a, b, lsem.at[i]) for i, (a, b) in enumerate(pieces)]
    for i, copy in enumerate(loads):
        if i != 2:
            copy.start()
    greet(
        [p.at(dx, dz) for dx, dz in MATES]
        + [p.at(0, 0, True)]
        + [p.peer(dh, dy) for dh, dy in PEERS]
        + [p.over(1, 0)]
    )
    gg = Gather(p, G, CUT, gss, grs)
    tg = Gather(p, TH, CUT, tss, trs)
    rg = Gather(p, R, CUT, rss, rrs)
    gathers = {"g": gg, "t": tg, "r": rg}
    sends = []

    def ship(src, dst, ss, rs, target):
        copy = remote(src, dst, ss, rs, target)
        copy.start()
        sends.append(copy)

    def land(ref, ss, rs):
        remote(ref, ref, ss, rs, p.at(0, 0, True)).wait_recv()

    loads[0].wait()
    gg.own()
    loads[1].wait()
    loads[2].start()

    pos = positions(ids[...], slots[...], counts)
    n = SB.shape[0] * 16
    row = lax.broadcasted_iota(jnp.int32, (n, 128), 0)
    pick = pos == (row // 16) * CAP + row % CAP
    scale = jnp.sum(jnp.where(pick, score[...], 0.0), axis=1, keepdims=True)
    pick = pick.astype(F32).astype(BF)
    wide = width // 2
    low = lax.broadcasted_iota(jnp.int32, (n, wide), 0) % 16 < 8
    grad = lax.broadcasted_iota(jnp.int32, (n, wide), 0) % 8 >= CAP
    vals_t = jnp.where(low, dot_nn(pick, TV[0, 0, :, 0:wide]), dot_nn(pick, TV[0, 0, :, wide:])) * scale
    vals_g = jnp.where(low, dot_nn(pick, G[t, :, 0:wide]), dot_nn(pick, G[t, :, wide:]))
    SB[...] = jnp.where(grad, vals_g, vals_t).astype(BF).reshape(SB.shape)
    for i, (dh, dy) in enumerate(PEERS):
        ship(SB.at[p.group(dh, dy)], RV.at[g], ass.at[i], ars.at[i], p.peer(dh, dy))
    RV[pl.ds(g, 1)] = SB[pl.ds(g, 1)]
    which = lax.broadcasted_iota(jnp.int32, (8, 128), 0)
    mine[...] = jnp.where(which == 0, pos.astype(F32), score[...])
    for i, (dx, dz) in enumerate(MATES):
        ship(mine, info.at[dx, (4 - dz) % 4], iss.at[i], irs.at[i], p.at(dx, dz))
    info[0, 0] = mine[...]
    acc_d[...] = jnp.zeros_like(acc_d)
    acc_gu[...] = jnp.zeros_like(acc_gu)

    def cols(i, size):
        return pl.ds(pl.multiple_of(i * size, size), size)

    def rows_own():
        for i, (dh, dy) in enumerate(PEERS):
            land(RV.at[p.group(dh, -dy)], ass.at[i], ars.at[i])
        rows = lax.broadcasted_iota(jnp.int32, (R.shape[1], n), 0)
        at = lax.broadcasted_iota(jnp.int32, (R.shape[1], n), 1)
        base = ((rows % 32) // CAP) * 16 + (rows // 32) * CAP + rows % CAP
        got = RV[...].reshape(n, wide)
        R[t, :, 0:wide] = dot_nn((at == base).astype(F32).astype(BF), got).astype(BF)
        R[t, :, wide:] = dot_nn((at == base + 8).astype(F32).astype(BF), got).astype(BF)
        rg.own()

    def shared_unit(i):
        gg.twin(*NEED[i])
        for k in (3, 4, 5):
            if loads[k] is not None:
                loads[k].wait()
                loads[k] = None
        j = p.chip(*CHIP[i])
        two = pl.ds(2 * j, 2)
        toks = pl.ds(pl.multiple_of(j * 256, 256), 256)
        h = dot_nt(G[two].reshape(256, width), wds_v[...])
        gate, up = dg_v[toks].astype(F32), du_v[toks].astype(F32)
        silu, slope = silu_parts(gate)
        dg, du = h * up * slope, h * silu
        dg_v[toks] = dg.astype(BF)
        du_v[toks] = du.astype(BF)
        dguT[j, 0:256] = dg.T.astype(BF)
        dguT[j, 256:512] = du.T.astype(BF)
        hidT[...] = (silu * up).T.astype(BF)

        def part(k, carry):
            cs = cols(k, 512)
            acc_d[:, cs] += dot_nn(hidT[...], G[two, :, cs].reshape(256, 512))
            return carry

        lax.fori_loop(0, width // 512, part, 0)

    slot_of, free = {}, [0, 1]

    def token_load(i):
        slot_of[i] = free.pop(0)
        tg.twin(*NEED[i])
        token_copy(i).start()

    def token_copy(i):
        j = p.chip(*CHIP[i])
        return pltpu.make_async_copy(TH.at[pl.ds(2 * j, 2)], TV.at[slot_of[i]], tsem.at[slot_of[i]])

    def token_unit(i):
        token_copy(i).wait()
        j, slot = p.chip(*CHIP[i]), slot_of[i]

        def part(k, carry):
            cs = cols(k, 512)
            acc_gu[:, cs] += dot_nn(dguT[j], TV[slot, :, :, cs].reshape(256, 512))
            return carry

        lax.fori_loop(0, width // 512, part, 0)
        free.append(slot)

    def r_unit(m):
        if m == 0:
            for i in range(8):
                rg.twin(*NEED[i])
            for k in (6, 7, 8):
                loads[k].wait()
        rin = R[8 * m : 8 * m + 8, 0:32].reshape(256, width)
        rgr = R[8 * m : 8 * m + 8, 32:64].reshape(256, width)
        gate, up = dot_nn(rin, wg_v[...]), dot_nn(rin, wu_v[...])
        h = dot_nt(rgr, wd_v[...])
        silu, slope = silu_parts(gate)
        dg, du = h * up * slope, h * silu
        dgb, dub = dg.astype(BF), du.astype(BF)
        at = pl.ds(m * 256, 256)
        rgu[at, 0:256] = dgb
        rgu[at, 256:512] = dub
        rguT[0:256, at] = dg.T.astype(BF)
        rguT[256:512, at] = du.T.astype(BF)
        rhT[:, at] = (silu * up).T.astype(BF)
        q = jnp.sum(dgb.astype(F32) * gate + dub.astype(F32) * up, axis=1, keepdims=True)
        hi = q.astype(BF).astype(F32)
        lane = lax.broadcasted_iota(jnp.int32, (256, 128), 1)
        tail = jnp.where(lane == 0, hi, jnp.where(lane == 1, q - hi, 0.0)).astype(BF)
        BP[4 * m : 4 * m + 4, :, :, width:] = tail.reshape(4, 2, 32, 128)

    def r_back():
        def part(k, carry):
            cs = cols(k, 512)
            out = dot_nt(rgu[:, 0:256], wg_v[cs]) + dot_nt(rgu[:, 256:512], wu_v[cs])
            BP[:, :, :, cs] = out.astype(BF).reshape(8, 2, 32, 512)
            return carry

        lax.fori_loop(0, width // 512, part, 0)
        ship(BP.at[:, 1 - c], BR, dss.at[0], drs.at[0], p.at(0, 0, True))

    keep = pltpu.make_async_copy(MS.at[g], BK.at[g], lsem.at[11])

    def r_send():
        land(BR, dss.at[0], drs.at[0])

        def part(k, carry):
            one = pl.ds(k, 1)
            BP[one, c] = (BP[one, c].astype(F32) + BR[one].astype(F32)).astype(BF)
            return carry

        lax.fori_loop(0, 8, part, 0)
        r0 = lax.broadcasted_iota(jnp.int32, (256, 256), 0)
        r1 = lax.broadcasted_iota(jnp.int32, (256, 256), 1)
        home, group = (r0 // CAP) % 8, r0 // 32
        held = jnp.where(group // 4 == p.xh, home, (home + 4) % 8)
        turn = (r1 == held * 32 + group * CAP + r0 % CAP).astype(F32).astype(BF)
        MS[...] = dot_nn(turn, BP[:, c].reshape(256, BP.shape[3])).astype(BF).reshape(MS.shape)
        for i, (dh, dy) in enumerate(PEERS):
            ship(MS.at[p.group(dh, dy)], BK.at[g], bss.at[i], brs.at[i], p.peer(dh, dy))
        keep.start()

    def w_copies(k, slot):
        return (
            pltpu.make_async_copy(WS.at[slot, 0], ggate.at[0, cols(k, 256)], wsem.at[slot, 0]),
            pltpu.make_async_copy(WS.at[slot, 1], gup.at[0, cols(k, 256)], wsem.at[slot, 1]),
            pltpu.make_async_copy(WS.at[slot, 2], gdown.at[0, :, cols(k, 256)], wsem.at[slot, 2]),
        )

    def w_unit(k, carry):
        slot = k % 2

        @pl.when(k >= 2)
        def _():
            for copy in w_copies(k - 2, slot):
                copy.wait()

        cs = cols(k, 256)
        gu = dot_nn(rguT[...], R[:, 0:32, cs].reshape(512, 256))
        WS[slot, 0] = gu[0:256].T.astype(BF)
        WS[slot, 1] = gu[256:512].T.astype(BF)
        WS[slot, 2] = dot_nn(rhT[...], R[:, 32:64, cs].reshape(512, 256)).astype(BF)
        for copy in w_copies(k, slot):
            copy.start()
        return carry

    def r_free():
        rg.finish()
        pl.semaphore_signal(credit, inc=1, device_id=p.at(0, 0, True), device_id_type=MESH)

    half = (pl.ds(0, 160), pl.ds(160, 160))

    def sum_first(V, VH, ss, rs, *dhs):
        for dh in dhs:
            for i, (s, d) in enumerate(DIRS):
                ship(V.at[:, p.group(dh, 2), half[i]], VH.at[dh, i], ss.at[dh, i], rs.at[dh, i], p.over(0, d))

    def sum_second(V, VH, VF, ss, rs, dh):
        for i, (s, d) in enumerate(DIRS):
            land(VH.at[dh, i], ss.at[dh, i], rs.at[dh, i])
            at = p.group(dh, d)
            for a in range(V.shape[0]):
                V[a, at, half[i]] = (V[a, at, half[i]].astype(F32) + VH[dh, i, a].astype(F32)).astype(BF)
            ship(V.at[:, at], VF.at[dh, i], ss.at[dh, 2 + i], rs.at[dh, 2 + i], p.over(0, d))

    def sum_total(V, VF, ss, rs, dh, a):
        return V[a, p.group(dh, 0)].astype(F32) + VF[dh, 0, a].astype(F32) + VF[dh, 1, a].astype(F32)

    def sum_third(V, VF, VX, ss, rs):
        for i in range(2):
            land(VF.at[1, i], ss.at[1, 2 + i], rs.at[1, 2 + i])
        at = p.group(1, 0)
        for a in range(V.shape[0]):
            V[a, at] = sum_total(V, VF, ss, rs, 1, a).astype(BF)
        ship(V.at[:, at], VX, ss.at[0, 4], rs.at[0, 4], p.over(1, 0))

    def sum_last(V, VF, VX, ss, rs):
        for i in range(2):
            land(VF.at[0, i], ss.at[0, 2 + i], rs.at[0, 2 + i])
        land(VX, ss.at[0, 4], rs.at[0, 4])
        return [sum_total(V, VF, ss, rs, 0, a) + VX[a].astype(F32) for a in range(V.shape[0])]

    def turn(acc, V):
        def part(k, carry):
            for a in range(V.shape[0]):
                block = acc[256 * a : 256 * a + 256, cols(k, 640)].T.astype(BF)
                V[a, 2 * k] = block[0:320]
                V[a, 2 * k + 1] = block[320:640]
            return carry

        lax.fori_loop(0, width // 640, part, 0)

    def down_last():
        total = sum_last(WD, DF, DX, hss, hrs)[0]
        gsd[...] = total.astype(BF)

    def weights_last():
        for a, total in enumerate(sum_last(W, WF, WX, wss, wrs)):
            gsg[a] = total.astype(BF)

    seen = set()

    def share(dx, dz):
        if "load" not in seen:
            seen.add("load")
            loads[9].wait()
            loads[10].wait()
        gg.finish((dx, dz))
        j = p.chip(dx, dz)
        toks = pl.ds(pl.multiple_of(j * 256, 256), 256)

        def part(k, carry):
            cs = cols(k, 512)
            out = dot_nt(dg_v[toks], wgs_v[cs]) + dot_nt(du_v[toks], wus_v[cs])
            G[pl.ds(2 * j, 2), :, cs] = out.astype(BF).reshape(2, 128, 512)
            return carry

        lax.fori_loop(0, width // 512, part, 0)

    def swap(dx, dz):
        if "credit" not in seen:
            seen.add("credit")
            pl.semaphore_wait(credit, 1)
        for h in range(2):
            at = 2 * (dx * 4 + dz) + h
            ship(G.at[p.member(dx, dz, True), pl.ds(64 * h, 64)], R.at[at], css.at[at], crs.at[at], p.at(0, 0, True))

    def picked(dx, dz):
        row = lax.broadcasted_iota(jnp.int32, (256, 128), 0)
        want = ((row // 32) * CAP + row % CAP).astype(F32)
        return (want == info[dx, dz, 0:1]) & ((row // CAP) % 8 == p.chip(dx, dz))

    def join(dx, dz):
        if "back" not in seen:
            seen.add("back")
            for i, (dh, dy) in enumerate(PEERS):
                land(BK.at[p.group(dh, -dy)], bss.at[i], brs.at[i])
            keep.wait()
            for i, (ax, az) in enumerate(MATES):
                land(info.at[ax, (4 - az) % 4], iss.at[i], irs.at[i])
            scale = jnp.zeros((256, 1), F32)
            for ax in range(2):
                for az in range(4):
                    scale += jnp.sum(jnp.where(picked(ax, az), info[ax, az, 1:2], 0.0), axis=1, keepdims=True)

            def weigh(k, carry):
                cs = cols(k, 512)
                BK[:, :, cs] = (BK[:, :, cs].reshape(256, 512).astype(F32) * scale).astype(BF).reshape(8, 32, 512)
                return carry

            lax.fori_loop(0, width // 512, weigh, 0)
        slot, me = dx * 4 + dz, p.member(dx, dz)
        pick = picked(dx, dz).astype(F32)
        pickT, pick = pick.T.astype(BF), pick.astype(BF)
        q = dot_tn(BK[:, :, width:].reshape(256, 128), pick)
        QS[dx, dz] = jnp.broadcast_to(q[0:1] + q[1:2], (8, 128))
        if (dx, dz) != (0, 0):
            i = MATES.index((dx, dz))
            ship(QS.at[dx, dz], QR.at[i], qss.at[i], qrs.at[i], p.at(dx, dz))
        for h in range(2):
            land(R.at[2 * slot + h], css.at[2 * slot + h], crs.at[2 * slot + h])

        def part(k, carry):
            cs = cols(k, 512)
            other = R[2 * slot : 2 * slot + 2, :, cs].reshape(128, 512)
            total = dot_nn(pickT, BK[:, :, cs].reshape(256, 512)) + G[me, :, cs].astype(F32) + other.astype(F32)
            G[me, :, cs] = total.astype(BF)
            return carry

        lax.fori_loop(0, width // 512, part, 0)

    colA, colB = pl.ds(0, RCUT), pl.ds(RCUT, width - RCUT)
    rowh = (pl.ds(0, 64), pl.ds(64, 64))

    def cols_of(lane):
        return colA if lane == 2 else colB

    def box(ref, lane, i, rows):
        return ref.at[lane, i, pl.ds(0, rows), pl.ds(0, RCUT if lane == 2 else width - RCUT)]

    def z_first(lane):
        me = p.member(lane % 2, 2)
        for i, (s, d) in enumerate(DIRS):
            ship(G.at[me, rowh[i], cols_of(lane)], box(ZH, lane, i, 64), zss.at[lane, i], zrs.at[lane, i], p.at(0, d))

    def z_second(lane):
        for i, (s, d) in enumerate(DIRS):
            me = p.member(lane % 2, d)
            ref = box(ZH, lane, i, 64)
            land(ref, zss.at[lane, i], zrs.at[lane, i])
            G[me, rowh[i], cols_of(lane)] = (
                G[me, rowh[i], cols_of(lane)].astype(F32) + ref[...].astype(F32)
            ).astype(BF)
            ship(G.at[me, :, cols_of(lane)], box(ZF, lane, i, 128), zss.at[lane, 2 + i], zrs.at[lane, 2 + i], p.at(0, d))

    def z_third(lane):
        for i in range(2):
            land(box(ZF, lane, i, 128), zss.at[lane, 2 + i], zrs.at[lane, 2 + i])
        return (
            G[p.member(lane % 2, 0), :, cols_of(lane)].astype(F32)
            + box(ZF, lane, 0, 128)[...].astype(F32)
            + box(ZF, lane, 1, 128)[...].astype(F32)
        )

    def x_send(dz):
        ship(G.at[p.member(1, dz), :, colA], XA.at[dz], xss.at[dz], xrs.at[dz], p.at(1, 0))

    def x_add(dz):
        land(XA.at[dz], xss.at[dz], xrs.at[dz])
        me = p.member(0, dz)
        G[me, :, colA] = (G[me, :, colA].astype(F32) + XA[dz].astype(F32)).astype(BF)

    def z_cross():
        me = p.member(1, 0)
        G[me, :, colB] = z_third(1).astype(BF)
        ship(G.at[me, :, colB], XB, xss.at[4], xrs.at[4], p.at(1, 0))

    def out_b():
        total = z_third(0)
        land(XB, xss.at[4], xrs.at[4])
        gtok[:, colB] = (total + XB[...].astype(F32)).astype(BF)

    def out_a():
        land(XA.at[0], xss.at[0], xrs.at[0])
        gtok[:, colA] = (z_third(2) + XA[0].astype(F32)).astype(BF)

    def tokens_own():
        loads[2].wait()
        tg.own()

    fixed = {
        "Rown": rows_own, "Town": tokens_own, "g2": gg.own_rest, "t2": tg.own_rest, "r2": rg.own_rest, "Rb": r_back, "Rs": r_send, "Rf": r_free,
        "Rw0": lambda: lax.fori_loop(0, 5, w_unit, 0), "Rw1": lambda: lax.fori_loop(5, 10, w_unit, 0),
        "D0": lambda: (turn(acc_d, WD), sum_first(WD, DH, hss, hrs, 1, 0)),
        "D1": lambda: (sum_second(WD, DH, DF, hss, hrs, 1), sum_second(WD, DH, DF, hss, hrs, 0)),
        "D2": lambda: sum_third(WD, DF, DX, hss, hrs), "D3": down_last,
        "W0": lambda: (turn(acc_gu, W), sum_first(W, WH, wss, wrs, 1)),
        "W0b": lambda: sum_first(W, WH, wss, wrs, 0),
        "W11": lambda: sum_second(W, WH, WF, wss, wrs, 1), "W10": lambda: sum_second(W, WH, WF, wss, wrs, 0),
        "W2": lambda: sum_third(W, WF, WX, wss, wrs), "W3": weights_last,
        "Z31": z_cross, "F0": out_b, "F2": out_a,
    }
    for step in ORDER:
        if step in fixed:
            fixed[step]()
        elif step[0] in gathers:
            gathers[step[0]].take(step[1:])
        elif step[:2] in ("Z1", "Z2"):
            (z_first if step[1] == "1" else z_second)(int(step[2]))
        else:
            unit = {"G": shared_unit, "L": token_load, "T": token_unit, "R": r_unit, "S": x_send, "X": x_add, "M": share, "N": swap, "J": join}
            unit[step[0]](*(int(k) for k in step[1:]))
    total = QS[0, 0]
    for i in range(len(MATES)):
        land(QR.at[i], qss.at[i], qrs.at[i])
        total = total + QR[i]
    gscore[...] = total[0:1] / score[...]
    for k in (8, 9):
        for copy in w_copies(k, k % 2):
            copy.wait()
    for copy in sends:
        copy.wait_send()
    gg.finish()
    tg.finish()


def store_kernel(gtok, gscore, gsg, gsd, ggate, gup, gdown, *rest):
    parts = (ggate, gup, gdown, gtok, gsg.at[0], gsg.at[1], gsd, gscore)
    outs, held, (first, second) = rest[:8], rest[8:16], rest[16:]
    loads = [pltpu.make_async_copy(a, b, first.at[i]) for i, (a, b) in enumerate(zip(parts, held))]
    stores = [pltpu.make_async_copy(a, b, second.at[i]) for i, (a, b) in enumerate(zip(held, outs))]
    for copy in loads:
        copy.start()
    for load, store in zip(loads, stores):
        load.wait()
        store.start()
    for copy in stores:
        copy.wait()


def shards(
    tokens, grad_out, route_score, expert_ids, slots, counts, shared_gate_pre, shared_up_pre,
    shared_w_gate, shared_w_up, shared_w_down, w_gate, w_up, w_down,
):
    tok_dev, width = tokens.shape
    ff = w_gate.shape[2]
    ids, slt, score = (a.reshape(1, tok_dev) for a in (expert_ids, slots, route_score))
    dma = pltpu.SemaphoreType.DMA
    wide, rows = width + 128, width // 8
    most = max(RCUT, width - RCUT)

    def vm(*shape, dtype=BF):
        return pltpu.VMEM(shape, dtype)

    def out(*shape, dtype=BF):
        return jax.ShapeDtypeStruct(shape, dtype)

    gtok, gscore, gsg, gsd, ggate, gup, gdown, _ = pl.pallas_call(
        kernel,
        out_shape=(
            out(tok_dev, width), out(1, tok_dev, dtype=F32), out(2, rows, ff), out(rows, ff),
            out(1, width, ff), out(1, width, ff), out(1, ff, width), out(16, tok_dev, width),
        ),
        in_specs=[ANY, ANY, VM, VM, SM, VM] + [ANY] * 8,
        out_specs=(VM, VM, VM, VM, ANY, ANY, ANY, ANY),
        scratch_shapes=[
            vm(16, tok_dev, width), vm(16, 64, width), vm(2, 2, tok_dev, width),
            vm(8, 16, width // 2), vm(8, 16, width // 2),
            vm(16 * tok_dev, ff), vm(16 * tok_dev, ff),
            vm(ff, width), vm(width, ff), vm(width, ff), vm(width, ff), vm(width, ff), vm(ff, width),
            vm(8, 2 * ff, 256), vm(ff, 256), vm(2 * ff, width, dtype=F32), vm(ff, width, dtype=F32),
            vm(512, 2 * ff), vm(2 * ff, 512), vm(ff, 512),
            vm(8, 2, 32, wide), vm(8, 32, wide), vm(8, 32, wide), vm(8, 32, wide),
            vm(2, 3, 256, 256),
            vm(2, 8, rows, ff), vm(2, 2, 2, rows // 2, ff), vm(2, 2, 2, rows, ff), vm(2, rows, ff),
            vm(1, 8, rows, ff), vm(2, 2, 1, rows // 2, ff), vm(2, 2, 1, rows, ff), vm(1, rows, ff),
            vm(4, tok_dev, RCUT), vm(3, 2, tok_dev // 2, most), vm(3, 2, tok_dev, most), vm(tok_dev, width - RCUT),
            vm(2, 4, 8, 128, dtype=F32), vm(8, 128, dtype=F32), vm(2, 4, 8, 128, dtype=F32), vm(7, 8, 128, dtype=F32),
            dma((12,)), dma((2,)), dma((2, 3)),
            dma((N_SLOT,)), dma((N_SLOT,)), dma((N_SLOT,)), dma((N_SLOT,)), dma((N_SLOT,)), dma((N_SLOT,)),
            dma((7,)), dma((7,)), dma((7,)), dma((7,)), dma((1,)), dma((1,)), dma((16,)), dma((16,)),
            dma((5,)), dma((5,)), dma((3, 4)), dma((3, 4)), dma((2, 5)), dma((2, 5)), dma((2, 5)), dma((2, 5)),
            dma((7,)), dma((7,)), dma((7,)), dma((7,)), pltpu.SemaphoreType.REGULAR,
        ],
        compiler_params=pltpu.CompilerParams(
            collective_id=0, has_side_effects=True, vmem_limit_bytes=63 << 20
        ),
    )(
        tokens, grad_out, ids, slt, counts, score, shared_gate_pre, shared_up_pre,
        shared_w_down, shared_w_gate, shared_w_up, w_gate, w_up, w_down,
    )
    shapes = (
        ((1, width, ff), BF), ((1, width, ff), BF), ((1, ff, width), BF), ((tok_dev, width), BF),
        ((rows, ff), BF), ((rows, ff), BF), ((rows, ff), BF), ((1, tok_dev), F32),
    )
    ggate, gup, gdown, gtok, gsg, gsu, gsd, gscore = pl.pallas_call(
        store_kernel,
        out_shape=tuple(out(*shape, dtype=dtype) for shape, dtype in shapes),
        in_specs=[ANY] * 7,
        out_specs=(ANY,) * 8,
        scratch_shapes=[vm(*shape, dtype=dtype) for shape, dtype in shapes] + [dma((8,)), dma((8,))],
        compiler_params=pltpu.CompilerParams(vmem_limit_bytes=63 << 20),
    )(gtok, gscore, gsg, gsd, ggate, gup, gdown)
    return (gtok, gscore.reshape(tok_dev), gsg, gsu, gsd.T, ggate, gup, gdown)


def solution(mesh):
    placed = (
        P(("grp", "tp"), None),
        P(("grp", "tp"), None),
        P(("grp", "tp")),
        P(("grp", "tp")),
        P(("grp", "tp")),
        P(("grp", "tp"), None),
        P("grp", "tp"),
        P("grp", "tp"),
        P(None, "tp"),
        P(None, "tp"),
        P("tp", None),
        P("grp", None, "tp"),
        P("grp", None, "tp"),
        P("grp", "tp", None),
    )
    return jax.shard_map(
        shards,
        mesh=mesh,
        in_specs=placed,
        out_specs=(
            P(("grp", "tp"), None),
            P(("grp", "tp")),
            P("grp", "tp"),
            P("grp", "tp"),
            P("tp", "grp"),
            P("grp", None, "tp"),
            P("grp", None, "tp"),
            P("grp", "tp", None),
        ),
        check_vma=False,
    )
```

```python
import functools

import jax
import jax.numpy as jnp
from jax import lax
from jax.experimental import pallas as pl
from jax.experimental.pallas import tpu as pltpu
from jax.sharding import PartitionSpec as P

CAP = 4
MESH = pl.DeviceIdType.MESH
BF, F32 = jnp.bfloat16, jnp.float32
ANY = pl.BlockSpec(memory_space=pl.ANY)
VM = pl.BlockSpec(memory_space=pltpu.VMEM)
SM = pl.BlockSpec(memory_space=pltpu.SMEM)
DIRS = (("+", 1), ("-", -1))


def dot_nn(a, b):
    return lax.dot_general(a, b, (((1,), (0,)), ((), ())), preferred_element_type=F32)


def dot_nt(a, b):
    return lax.dot_general(a, b, (((1,), (1,)), ((), ())), preferred_element_type=F32)


def dot_tn(a, b):
    return lax.dot_general(a, b, (((0,), (0,)), ((), ())), preferred_element_type=F32)


class Place:
    def __init__(self):
        self.g = lax.axis_index("grp")
        self.t = lax.axis_index("tp")
        self.xh, self.y = self.g // 4, self.g % 4
        self.xl, self.z, self.c = self.t // 8, (self.t // 2) % 4, self.t % 2

    def chip(self, dx, dz):
        return ((self.xl + dx) % 2) * 4 + (self.z + dz + 4) % 4

    def member(self, dx, dz, other=False):
        core = 1 - self.c if other else self.c
        return self.chip(dx, dz) * 2 + core

    def at(self, dx, dz, other=False):
        return (self.g, self.member(dx, dz, other))

    def group(self, dh, dy):
        return ((self.xh + dh) % 2) * 4 + (self.y + dy + 4) % 4

    def over(self, dh, dy):
        return (self.group(dh, dy), self.t)

    def peer(self, dh, dy):
        return (self.group(dh, dy), (self.t + 8 * dh) % 16)


def greet(targets):
    barrier = pltpu.get_barrier_semaphore()
    for target in targets:
        pl.semaphore_signal(barrier, inc=1, device_id=target, device_id_type=MESH)
    pl.semaphore_wait(barrier, len(targets))


def remote(src, dst, ss, rs, target):
    return pltpu.make_async_remote_copy(
        src_ref=src, dst_ref=dst, send_sem=ss, recv_sem=rs, device_id=target, device_id_type=MESH
    )


ARRIVE = {"xB": (1, 0, None, "B"), "xA0": (1, 0, None, "A")}
for _s, _d in DIRS:
    _h = 0 if _d > 0 else 1
    ARRIVE["zA" + _s] = (0, -_d, None, "A")
    ARRIVE["zB" + _s] = (0, -_d, None, "B")
    ARRIVE["zX" + _s] = (1, -_d, None, "B")
    ARRIVE["hA" + _s] = (0, 2, _h, "A")
    ARRIVE["hB" + _s] = (0, 2, _h, "B")
    ARRIVE["hX" + _s] = (1, 2, _h, "B")
    ARRIVE["xA" + _s] = (1, -_d, None, "A")
    ARRIVE["xh" + _s] = (1, 2, _h, "A")
SLOT = {name: i for i, name in enumerate(ARRIVE)}
N_ICI = len(SLOT)
N_SLOT = 2 * N_ICI + 1


class Gather:
    def __init__(self, place, buf, cut, ss, rs):
        self.p, self.buf, self.cut, self.ss, self.rs = place, buf, cut, ss, rs
        self.rows, self.width = buf.shape[1], buf.shape[2]
        self.sent = {}

    def ref(self, member, half, part):
        rows = pl.ds(0, self.rows) if half is None else pl.ds(half * (self.rows // 2), self.rows // 2)
        cols = {
            None: pl.ds(0, self.width),
            "A": pl.ds(0, self.cut),
            "B": pl.ds(self.cut, self.width - self.cut),
        }[part]
        return self.buf.at[member, rows, cols]

    def send(self, slot, chip, half, part, target):
        ref = self.ref(self.p.member(*chip), half, part)
        copy = remote(ref, ref, self.ss.at[slot], self.rs.at[slot], target)
        copy.start()
        self.sent.setdefault((chip[0], chip[1] % 4), []).append(copy)

    def own(self):
        p, me = self.p, (0, 0)
        for s, d in DIRS:
            self.send(SLOT["zA" + s], me, None, "A", p.at(0, d))
        self.send(SLOT["xB"], me, None, "B", p.at(1, 0))
        self.send(2 * N_ICI, me, None, None, p.at(0, 0, True))

    def own_rest(self):
        p, me = self.p, (0, 0)
        for s, d in DIRS:
            self.send(SLOT["zB" + s], me, None, "B", p.at(0, d))
        self.send(SLOT["xA0"], me, None, "A", p.at(1, 0))

    def take(self, *names):
        for name in names:
            self.take_one(name)

    def take_one(self, name):
        p = self.p
        dx, dz, half, part = ARRIVE[name]
        member = (dx, dz)
        ref = self.ref(p.member(dx, dz), half, part)
        remote(ref, ref, self.ss.at[SLOT[name]], self.rs.at[SLOT[name]], p.at(1, 0)).wait_recv()
        kind, s = name[:2], name[2:]
        if name == "xB":
            for s2, d in DIRS:
                self.send(SLOT["zX" + s2], member, None, "B", p.at(0, d))
        if kind[0] == "z":
            d = 1 if s == "+" else -1
            if kind == "zA":
                self.send(SLOT["xA" + s], member, None, "A", p.at(1, 0))
            self.send(SLOT["h" + kind[1] + s], member, 0 if d > 0 else 1, part, p.at(0, d))
        if kind == "hA":
            self.send(SLOT["xh" + s], member, half, "A", p.at(1, 0))
        self.send(N_ICI + SLOT[name], member, half, part, p.at(0, 0, True))

    def twin(self, *names):
        for name in names:
            if name == "own":
                slot, ref = 2 * N_ICI, self.ref(self.p.member(0, 0, True), None, None)
            else:
                dx, dz, half, part = ARRIVE[name]
                slot, ref = N_ICI + SLOT[name], self.ref(self.p.member(dx, dz, True), half, part)
            remote(ref, ref, self.ss.at[slot], self.rs.at[slot], self.p.at(0, 0, True)).wait_recv()

    def finish(self, chip=None):
        for key in list(self.sent) if chip is None else [(chip[0], chip[1] % 4)]:
            for copy in self.sent.pop(key, []):
                copy.wait_send()


CHIP = ((0, 0), (1, 0), (0, -1), (0, 1), (1, -1), (1, 1), (0, 2), (1, 2))
NEED = (
    ("own",),
    ("xB", "xA0"),
    ("zA+", "zB+"),
    ("zA-", "zB-"),
    ("zX+", "xA+"),
    ("zX-", "xA-"),
    ("hA+", "hA-", "hB+", "hB-"),
    ("hX+", "hX-", "xh+", "xh-"),
)
PEERS = [(dh, dy) for dh in range(2) for dy in range(4) if (dh, dy) != (0, 0)]
MATES = [(dx, dz) for dx in range(2) for dz in range(4) if (dx, dz) != (0, 0)]
CUT = 1152
RCUT = 1024
ORDER = (
    "G0", "g2", "Rown", "r2", "rzA+", "rzA-", "rxB", "M00", "gzA+", "gzB-", "gzA-", "gzB+", "rhA-",
    "rzB-", "rzB+", "gxA0", "rxA-", "gxB", "rzX-", "rzX+", "rhA+", "G1", "G2", "rxA+", "rxA0", "ghA-",
    "Town", "t2", "rhB-", "G3", "ghA+", "ghB+", "rhX+", "rxh+", "ghB-", "rxh-", "rhB+", "rhX-", "R0",
    "R1", "Rb", "Rh", "M03", "G6", "gzX+", "gxA+", "gzX-", "gxA-", "Rs", "tzA-", "tzA+", "gxh-", "Rf",
    "M02", "M10", "N10", "M01", "tzB+", "N01", "tzB-", "gxh+", "G4", "N00", "ghX+", "N02", "G5", "txB",
    "N03", "L1", "M11", "ghX-", "txA0", "thA+", "N11", "M13", "N13", "thB-", "T1", "J02", "L0", "thA-",
    "Z10", "G7", "D0", "M12", "N12", "J11", "S1", "tzX+", "txA+", "tzX-", "J13", "txA-", "T0", "thB+",
    "J12", "Z11", "S2", "D1", "txh+", "L2", "J00", "txh-", "thX-", "thX+", "S3", "T2", "L3", "Z21",
    "T3", "D2", "W0", "J10", "X2", "Z12", "S0", "J03", "J01", "X1", "W0b", "W11", "X3", "Z20", "Z31",
    "D3", "Rw0", "Rw1", "Z22", "W10", "W2", "F0", "F2", "W3",
)


def positions(ids, slots, counts):
    own = jnp.zeros(ids.shape, jnp.int32)
    experts = counts.shape[1]
    for e in range(experts):
        own = own + jnp.where(ids == e, counts[0, e], 0)
    live = (ids < experts) & (slots < own)
    return jnp.where(live, ids * CAP + slots, -1)


def silu_parts(gate):
    sigma = jax.nn.sigmoid(gate)
    return gate * sigma, sigma * (1.0 + gate * (1.0 - sigma))


def kernel(
    tok, grd, ids, slots, counts, score, gpre, upre, wds, wgs, wus, wg, wu, wd,
    gtok, gscore, gsg, gsd, ggate, gup, gdown, TH, RH,
    G, R, TV, SB, RV, dg_v, du_v, wds_v, wgs_v, wus_v, wg_v, wu_v, wd_v, dguT, hidT, acc_gu, acc_d,
    rgu, rguT, rhT, BP, BR, MS, BK, WS, RS, W, WH, WF, WX, WD, DH, DF, DX,
    XA, ZH, ZF, XB, info, mine, QS, QR,
    lsem, tsem, wsem, rsem, gss, grs, tss, trs, rss, rrs, ass, ars, bss, brs, dss, drs, css, crs,
    xss, xrs, zss, zrs, wss, wrs, hss, hrs, iss, irs, qss, qrs, credit,
):
    p = Place()
    g, t, c = p.g, p.t, p.c
    width = gtok.shape[1]
    pieces = ((grd, G.at[t]), (tok, TV.at[0, 0]), (TV.at[0, 0], TH.at[t]), (wds, wds_v), (gpre, dg_v), (upre, du_v),
              (wg.at[0], wg_v), (wu.at[0], wu_v), (wd.at[0], wd_v), (wgs, wgs_v), (wus, wus_v))
    loads = [pltpu.make_async_copy(a, b, lsem.at[i]) for i, (a, b) in enumerate(pieces)]
    for i, copy in enumerate(loads):
        if i != 2:
            copy.start()
    greet(
        [p.at(dx, dz) for dx, dz in MATES]
        + [p.at(0, 0, True)]
        + [p.peer(dh, dy) for dh, dy in PEERS]
        + [p.over(1, 0)]
    )
    gg = Gather(p, G, CUT, gss, grs)
    tg = Gather(p, TH, CUT, tss, trs)
    rg = Gather(p, R, CUT, rss, rrs)
    gathers = {"g": gg, "t": tg, "r": rg}
    sends = []

    def ship(src, dst, ss, rs, target):
        copy = remote(src, dst, ss, rs, target)
        copy.start()
        sends.append(copy)

    def land(ref, ss, rs):
        remote(ref, ref, ss, rs, p.at(0, 0, True)).wait_recv()

    loads[0].wait()
    gg.own()
    loads[1].wait()
    loads[2].start()

    pos = positions(ids[...], slots[...], counts)
    n = SB.shape[0] * 16
    row = lax.broadcasted_iota(jnp.int32, (n, 128), 0)
    pick = pos == (row // 16) * CAP + row % CAP
    scale = jnp.sum(jnp.where(pick, score[...], 0.0), axis=1, keepdims=True)
    pick = pick.astype(F32).astype(BF)
    wide = width // 2
    low = lax.broadcasted_iota(jnp.int32, (n, wide), 0) % 16 < 8
    grad = lax.broadcasted_iota(jnp.int32, (n, wide), 0) % 8 >= CAP
    vals_t = jnp.where(low, dot_nn(pick, TV[0, 0, :, 0:wide]), dot_nn(pick, TV[0, 0, :, wide:])) * scale
    vals_g = jnp.where(low, dot_nn(pick, G[t, :, 0:wide]), dot_nn(pick, G[t, :, wide:]))
    SB[...] = jnp.where(grad, vals_g, vals_t).astype(BF).reshape(SB.shape)
    for i, (dh, dy) in enumerate(PEERS):
        ship(SB.at[p.group(dh, dy)], RV.at[g], ass.at[i], ars.at[i], p.peer(dh, dy))
    RV[pl.ds(g, 1)] = SB[pl.ds(g, 1)]
    which = lax.broadcasted_iota(jnp.int32, (8, 128), 0)
    mine[...] = jnp.where(which == 0, pos.astype(F32), score[...])
    for i, (dx, dz) in enumerate(MATES):
        ship(mine, info.at[dx, (4 - dz) % 4], iss.at[i], irs.at[i], p.at(dx, dz))
    info[0, 0] = mine[...]
    acc_d[...] = jnp.zeros_like(acc_d)
    acc_gu[...] = jnp.zeros_like(acc_gu)

    def cols(i, size):
        return pl.ds(pl.multiple_of(i * size, size), size)

    def rows_own():
        for i, (dh, dy) in enumerate(PEERS):
            land(RV.at[p.group(dh, -dy)], ass.at[i], ars.at[i])
        rows = lax.broadcasted_iota(jnp.int32, (R.shape[1], n), 0)
        at = lax.broadcasted_iota(jnp.int32, (R.shape[1], n), 1)
        base = ((rows % 32) // CAP) * 16 + (rows // 32) * CAP + rows % CAP
        got = RV[...].reshape(n, wide)
        R[t, :, 0:wide] = dot_nn((at == base).astype(F32).astype(BF), got).astype(BF)
        R[t, :, wide:] = dot_nn((at == base + 8).astype(F32).astype(BF), got).astype(BF)
        rg.own()

    def shared_unit(i):
        gg.twin(*NEED[i])
        for k in (3, 4, 5):
            if loads[k] is not None:
                loads[k].wait()
                loads[k] = None
        j = p.chip(*CHIP[i])
        two = pl.ds(2 * j, 2)
        toks = pl.ds(pl.multiple_of(j * 256, 256), 256)
        h = dot_nt(G[two].reshape(256, width), wds_v[...])
        gate, up = dg_v[toks].astype(F32), du_v[toks].astype(F32)
        silu, slope = silu_parts(gate)
        dg, du = h * up * slope, h * silu
        dg_v[toks] = dg.astype(BF)
        du_v[toks] = du.astype(BF)
        dguT[j, 0:256] = dg.T.astype(BF)
        dguT[j, 256:512] = du.T.astype(BF)
        hidT[...] = (silu * up).T.astype(BF)

        def part(k, carry):
            cs = cols(k, 512)
            acc_d[:, cs] += dot_nn(hidT[...], G[two, :, cs].reshape(256, 512))
            return carry

        lax.fori_loop(0, width // 512, part, 0)

    def token_copy(i):
        j = p.chip(*CHIP[i])
        return pltpu.make_async_copy(TH.at[pl.ds(2 * j, 2)], TV.at[i % 2], tsem.at[i % 2])

    def token_load(i):
        for k in (2 * i, 2 * i + 1):
            tg.twin(*NEED[k])
            token_copy(k).start()

    def token_unit(i):
        token_copy(2 * i).wait()
        token_copy(2 * i + 1).wait()
        j, k = p.chip(*CHIP[2 * i]), p.chip(*CHIP[2 * i + 1])

        def part(n, carry):
            cs = cols(n, 512)
            acc_gu[:, cs] += dot_nn(dguT[j], TV[0, :, :, cs].reshape(256, 512)) + dot_nn(
                dguT[k], TV[1, :, :, cs].reshape(256, 512)
            )
            return carry

        lax.fori_loop(0, width // 512, part, 0)

    def r_unit(m):
        if m == 0:
            for i in range(8):
                rg.twin(*NEED[i])
            for k in (6, 7, 8):
                loads[k].wait()
        rin = R[8 * m : 8 * m + 8, 0:32].reshape(256, width)
        rgr = R[8 * m : 8 * m + 8, 32:64].reshape(256, width)
        gate, up = dot_nn(rin, wg_v[...]), dot_nn(rin, wu_v[...])
        h = dot_nt(rgr, wd_v[...])
        silu, slope = silu_parts(gate)
        dg, du = h * up * slope, h * silu
        dgb, dub = dg.astype(BF), du.astype(BF)
        at = pl.ds(m * 256, 256)
        rgu[at, 0:256] = dgb
        rgu[at, 256:512] = dub
        rguT[0:256, at] = dg.T.astype(BF)
        rguT[256:512, at] = du.T.astype(BF)
        rhT[:, at] = (silu * up).T.astype(BF)
        q = jnp.sum(dgb.astype(F32) * gate + dub.astype(F32) * up, axis=1, keepdims=True)
        hi = q.astype(BF).astype(F32)
        lane = lax.broadcasted_iota(jnp.int32, (256, 128), 1)
        tail = jnp.where(lane == 0, hi, jnp.where(lane == 1, q - hi, 0.0)).astype(BF)
        BP[4 * m : 4 * m + 4, :, :, width:] = tail.reshape(4, 2, 32, 128)

    def r_back():
        def part(k, carry):
            cs = cols(k, 512)
            out = dot_nt(rgu[:, 0:256], wg_v[cs]) + dot_nt(rgu[:, 256:512], wu_v[cs])
            BP[:, :, :, cs] = out.astype(BF).reshape(8, 2, 32, 512)
            return carry

        lax.fori_loop(0, width // 512, part, 0)
        ship(BP.at[:, 1 - c], BR, dss.at[0], drs.at[0], p.at(0, 0, True))

    keep = pltpu.make_async_copy(MS.at[g], BK.at[g], lsem.at[11])

    def r_send():
        land(BR, dss.at[0], drs.at[0])

        def part(k, carry):
            one = pl.ds(k, 1)
            BP[one, c] = (BP[one, c].astype(F32) + BR[one].astype(F32)).astype(BF)
            return carry

        lax.fori_loop(0, 8, part, 0)
        r0 = lax.broadcasted_iota(jnp.int32, (256, 256), 0)
        r1 = lax.broadcasted_iota(jnp.int32, (256, 256), 1)
        home, group = (r0 // CAP) % 8, r0 // 32
        held = jnp.where(group // 4 == p.xh, home, (home + 4) % 8)
        turn = (r1 == held * 32 + group * CAP + r0 % CAP).astype(F32).astype(BF)
        MS[...] = dot_nn(turn, BP[:, c].reshape(256, BP.shape[3])).astype(BF).reshape(MS.shape)
        for i, (dh, dy) in enumerate(PEERS):
            ship(MS.at[p.group(dh, dy)], BK.at[g], bss.at[i], brs.at[i], p.peer(dh, dy))
        keep.start()

    def w_copies(k, slot):
        return (
            pltpu.make_async_copy(WS.at[slot, 0], ggate.at[0, cols(k, 256)], wsem.at[slot, 0]),
            pltpu.make_async_copy(WS.at[slot, 1], gup.at[0, cols(k, 256)], wsem.at[slot, 1]),
            pltpu.make_async_copy(WS.at[slot, 2], gdown.at[0, :, cols(k, 256)], wsem.at[slot, 2]),
        )

    def w_load(k, slot):
        return pltpu.make_async_copy(RH.at[:, :, cols(k, 256)], RS.at[slot], rsem.at[slot])

    def w_unit(k, carry):
        slot = k % 2
        w_load(k, slot).wait()

        @pl.when(k + 1 < width // 256)
        def _():
            w_load(k + 1, 1 - slot).start()

        @pl.when(k >= 2)
        def _():
            for copy in w_copies(k - 2, slot):
                copy.wait()

        gu = dot_nn(rguT[...], RS[slot, :, 0:32].reshape(512, 256))
        WS[slot, 0] = gu[0:256].T.astype(BF)
        WS[slot, 1] = gu[256:512].T.astype(BF)
        WS[slot, 2] = dot_nn(rhT[...], RS[slot, :, 32:64].reshape(512, 256)).astype(BF)
        for copy in w_copies(k, slot):
            copy.start()
        return carry

    rows_out = pltpu.make_async_copy(R, RH, lsem.at[12])

    def r_free():
        rg.finish()
        rows_out.wait()
        pl.semaphore_signal(credit, inc=1, device_id=p.at(0, 0, True), device_id_type=MESH)

    half = (pl.ds(0, 160), pl.ds(160, 160))

    def sum_first(V, VH, ss, rs, *dhs):
        for dh in dhs:
            for i, (s, d) in enumerate(DIRS):
                ship(V.at[:, p.group(dh, 2), half[i]], VH.at[dh, i], ss.at[dh, i], rs.at[dh, i], p.over(0, d))

    def sum_second(V, VH, VF, ss, rs, dh):
        for i, (s, d) in enumerate(DIRS):
            land(VH.at[dh, i], ss.at[dh, i], rs.at[dh, i])
            at = p.group(dh, d)
            for a in range(V.shape[0]):
                V[a, at, half[i]] = (V[a, at, half[i]].astype(F32) + VH[dh, i, a].astype(F32)).astype(BF)
            ship(V.at[:, at], VF.at[dh, i], ss.at[dh, 2 + i], rs.at[dh, 2 + i], p.over(0, d))

    def sum_total(V, VF, ss, rs, dh, a):
        return V[a, p.group(dh, 0)].astype(F32) + VF[dh, 0, a].astype(F32) + VF[dh, 1, a].astype(F32)

    def sum_third(V, VF, VX, ss, rs):
        for i in range(2):
            land(VF.at[1, i], ss.at[1, 2 + i], rs.at[1, 2 + i])
        at = p.group(1, 0)
        for a in range(V.shape[0]):
            V[a, at] = sum_total(V, VF, ss, rs, 1, a).astype(BF)
        ship(V.at[:, at], VX, ss.at[0, 4], rs.at[0, 4], p.over(1, 0))

    def sum_last(V, VF, VX, ss, rs):
        for i in range(2):
            land(VF.at[0, i], ss.at[0, 2 + i], rs.at[0, 2 + i])
        land(VX, ss.at[0, 4], rs.at[0, 4])
        return [sum_total(V, VF, ss, rs, 0, a) + VX[a].astype(F32) for a in range(V.shape[0])]

    def turn(acc, V):
        def part(k, carry):
            for a in range(V.shape[0]):
                block = acc[256 * a : 256 * a + 256, cols(k, 640)].T.astype(BF)
                V[a, 2 * k] = block[0:320]
                V[a, 2 * k + 1] = block[320:640]
            return carry

        lax.fori_loop(0, width // 640, part, 0)

    def down_last():
        total = sum_last(WD, DF, DX, hss, hrs)[0]
        gsd[...] = total.astype(BF)

    def weights_last():
        for a, total in enumerate(sum_last(W, WF, WX, wss, wrs)):
            gsg[a] = total.astype(BF)

    seen = set()

    def share(dx, dz):
        if "load" not in seen:
            seen.add("load")
            loads[9].wait()
            loads[10].wait()
        gg.finish((dx, dz))
        j = p.chip(dx, dz)
        toks = pl.ds(pl.multiple_of(j * 256, 256), 256)

        def part(k, carry):
            cs = cols(k, 512)
            out = dot_nt(dg_v[toks], wgs_v[cs]) + dot_nt(du_v[toks], wus_v[cs])
            G[pl.ds(2 * j, 2), :, cs] = out.astype(BF).reshape(2, 128, 512)
            return carry

        lax.fori_loop(0, width // 512, part, 0)

    def swap(dx, dz):
        if "credit" not in seen:
            seen.add("credit")
            pl.semaphore_wait(credit, 1)
        for h in range(2):
            at = 2 * (dx * 4 + dz) + h
            ship(G.at[p.member(dx, dz, True), pl.ds(64 * h, 64)], R.at[at], css.at[at], crs.at[at], p.at(0, 0, True))

    def picked(dx, dz):
        row = lax.broadcasted_iota(jnp.int32, (256, 128), 0)
        want = ((row // 32) * CAP + row % CAP).astype(F32)
        return (want == info[dx, dz, 0:1]) & ((row // CAP) % 8 == p.chip(dx, dz))

    def join(dx, dz):
        if "back" not in seen:
            seen.add("back")
            for i, (dh, dy) in enumerate(PEERS):
                land(BK.at[p.group(dh, -dy)], bss.at[i], brs.at[i])
            keep.wait()
            for i, (ax, az) in enumerate(MATES):
                land(info.at[ax, (4 - az) % 4], iss.at[i], irs.at[i])
            scale = jnp.zeros((256, 1), F32)
            for ax in range(2):
                for az in range(4):
                    scale += jnp.sum(jnp.where(picked(ax, az), info[ax, az, 1:2], 0.0), axis=1, keepdims=True)

            def weigh(k, carry):
                cs = cols(k, 512)
                BK[:, :, cs] = (BK[:, :, cs].reshape(256, 512).astype(F32) * scale).astype(BF).reshape(8, 32, 512)
                return carry

            lax.fori_loop(0, width // 512, weigh, 0)
        slot, me = dx * 4 + dz, p.member(dx, dz)
        pick = picked(dx, dz).astype(F32)
        pickT, pick = pick.T.astype(BF), pick.astype(BF)
        q = dot_tn(BK[:, :, width:].reshape(256, 128), pick)
        QS[dx, dz] = jnp.broadcast_to(q[0:1] + q[1:2], (8, 128))
        if (dx, dz) != (0, 0):
            i = MATES.index((dx, dz))
            ship(QS.at[dx, dz], QR.at[i], qss.at[i], qrs.at[i], p.at(dx, dz))
        for h in range(2):
            land(R.at[2 * slot + h], css.at[2 * slot + h], crs.at[2 * slot + h])

        def part(k, carry):
            cs = cols(k, 512)
            other = R[2 * slot : 2 * slot + 2, :, cs].reshape(128, 512)
            total = dot_nn(pickT, BK[:, :, cs].reshape(256, 512)) + G[me, :, cs].astype(F32) + other.astype(F32)
            G[me, :, cs] = total.astype(BF)
            return carry

        lax.fori_loop(0, width // 512, part, 0)

    colA, colB = pl.ds(0, RCUT), pl.ds(RCUT, width - RCUT)
    rowh = (pl.ds(0, 64), pl.ds(64, 64))

    def cols_of(lane):
        return colA if lane == 2 else colB

    def box(ref, lane, i, rows):
        return ref.at[lane, i, pl.ds(0, rows), pl.ds(0, RCUT if lane == 2 else width - RCUT)]

    def z_first(lane):
        me = p.member(lane % 2, 2)
        for i, (s, d) in enumerate(DIRS):
            ship(G.at[me, rowh[i], cols_of(lane)], box(ZH, lane, i, 64), zss.at[lane, i], zrs.at[lane, i], p.at(0, d))

    def z_second(lane):
        for i, (s, d) in enumerate(DIRS):
            me = p.member(lane % 2, d)
            ref = box(ZH, lane, i, 64)
            land(ref, zss.at[lane, i], zrs.at[lane, i])
            G[me, rowh[i], cols_of(lane)] = (
                G[me, rowh[i], cols_of(lane)].astype(F32) + ref[...].astype(F32)
            ).astype(BF)
            ship(G.at[me, :, cols_of(lane)], box(ZF, lane, i, 128), zss.at[lane, 2 + i], zrs.at[lane, 2 + i], p.at(0, d))

    def z_third(lane):
        for i in range(2):
            land(box(ZF, lane, i, 128), zss.at[lane, 2 + i], zrs.at[lane, 2 + i])
        return (
            G[p.member(lane % 2, 0), :, cols_of(lane)].astype(F32)
            + box(ZF, lane, 0, 128)[...].astype(F32)
            + box(ZF, lane, 1, 128)[...].astype(F32)
        )

    def x_send(dz):
        ship(G.at[p.member(1, dz), :, colA], XA.at[dz], xss.at[dz], xrs.at[dz], p.at(1, 0))

    def x_add(dz):
        land(XA.at[dz], xss.at[dz], xrs.at[dz])
        me = p.member(0, dz)
        G[me, :, colA] = (G[me, :, colA].astype(F32) + XA[dz].astype(F32)).astype(BF)

    def z_cross():
        me = p.member(1, 0)
        G[me, :, colB] = z_third(1).astype(BF)
        ship(G.at[me, :, colB], XB, xss.at[4], xrs.at[4], p.at(1, 0))

    def out_b():
        total = z_third(0)
        land(XB, xss.at[4], xrs.at[4])
        gtok[:, colB] = (total + XB[...].astype(F32)).astype(BF)

    def out_a():
        land(XA.at[0], xss.at[0], xrs.at[0])
        gtok[:, colA] = (z_third(2) + XA[0].astype(F32)).astype(BF)

    def tokens_own():
        loads[2].wait()
        tg.own()

    fixed = {
        "Rown": rows_own, "Town": tokens_own, "g2": gg.own_rest, "t2": tg.own_rest, "r2": rg.own_rest, "Rb": r_back, "Rs": r_send, "Rf": r_free,
        "Rh": rows_out.start,
        "Rw0": lambda: (w_load(0, 0).start(), lax.fori_loop(0, 5, w_unit, 0)), "Rw1": lambda: lax.fori_loop(5, 10, w_unit, 0),
        "D0": lambda: (turn(acc_d, WD), sum_first(WD, DH, hss, hrs, 1, 0)),
        "D1": lambda: (sum_second(WD, DH, DF, hss, hrs, 1), sum_second(WD, DH, DF, hss, hrs, 0)),
        "D2": lambda: sum_third(WD, DF, DX, hss, hrs), "D3": down_last,
        "W0": lambda: (turn(acc_gu, W), sum_first(W, WH, wss, wrs, 1)),
        "W0b": lambda: sum_first(W, WH, wss, wrs, 0),
        "W11": lambda: sum_second(W, WH, WF, wss, wrs, 1), "W10": lambda: sum_second(W, WH, WF, wss, wrs, 0),
        "W2": lambda: sum_third(W, WF, WX, wss, wrs), "W3": weights_last,
        "Z31": z_cross, "F0": out_b, "F2": out_a,
    }
    for step in ORDER:
        if step in fixed:
            fixed[step]()
        elif step[0] in gathers:
            gathers[step[0]].take(step[1:])
        elif step[:2] in ("Z1", "Z2"):
            (z_first if step[1] == "1" else z_second)(int(step[2]))
        else:
            unit = {"G": shared_unit, "L": token_load, "T": token_unit, "R": r_unit, "S": x_send, "X": x_add, "M": share, "N": swap, "J": join}
            unit[step[0]](*(int(k) for k in step[1:]))
    total = QS[0, 0]
    for i in range(len(MATES)):
        land(QR.at[i], qss.at[i], qrs.at[i])
        total = total + QR[i]
    gscore[...] = total[0:1] / score[...]
    for k in (8, 9):
        for copy in w_copies(k, k % 2):
            copy.wait()
    for copy in sends:
        copy.wait_send()
    gg.finish()
    tg.finish()


def store_kernel(gtok, gscore, gsg, gsd, ggate, gup, gdown, *rest):
    parts = (ggate, gup, gdown, gtok, gsg.at[0], gsg.at[1], gsd, gscore)
    outs, held, (first, second) = rest[:8], rest[8:16], rest[16:]
    loads = [pltpu.make_async_copy(a, b, first.at[i]) for i, (a, b) in enumerate(zip(parts, held))]
    stores = [pltpu.make_async_copy(a, b, second.at[i]) for i, (a, b) in enumerate(zip(held, outs))]
    for copy in loads:
        copy.start()
    for load, store in zip(loads, stores):
        load.wait()
        store.start()
    for copy in stores:
        copy.wait()


def shards(
    tokens, grad_out, route_score, expert_ids, slots, counts, shared_gate_pre, shared_up_pre,
    shared_w_gate, shared_w_up, shared_w_down, w_gate, w_up, w_down,
):
    tok_dev, width = tokens.shape
    ff = w_gate.shape[2]
    ids, slt, score = (a.reshape(1, tok_dev) for a in (expert_ids, slots, route_score))
    dma = pltpu.SemaphoreType.DMA
    wide, rows = width + 128, width // 8
    most = max(RCUT, width - RCUT)

    def vm(*shape, dtype=BF):
        return pltpu.VMEM(shape, dtype)

    def out(*shape, dtype=BF):
        return jax.ShapeDtypeStruct(shape, dtype)

    gtok, gscore, gsg, gsd, ggate, gup, gdown, _, _ = pl.pallas_call(
        kernel,
        out_shape=(
            out(tok_dev, width), out(1, tok_dev, dtype=F32), out(2, rows, ff), out(rows, ff),
            out(1, width, ff), out(1, width, ff), out(1, ff, width), out(16, tok_dev, width),
            out(16, 64, width),
        ),
        in_specs=[ANY, ANY, VM, VM, SM, VM] + [ANY] * 8,
        out_specs=(VM, VM, VM, VM, ANY, ANY, ANY, ANY, ANY),
        scratch_shapes=[
            vm(16, tok_dev, width), vm(16, 64, width), vm(2, 2, tok_dev, width),
            vm(8, 16, width // 2), vm(8, 16, width // 2),
            vm(16 * tok_dev, ff), vm(16 * tok_dev, ff),
            vm(ff, width), vm(width, ff), vm(width, ff), vm(width, ff), vm(width, ff), vm(ff, width),
            vm(8, 2 * ff, 256), vm(ff, 256), vm(2 * ff, width, dtype=F32), vm(ff, width, dtype=F32),
            vm(512, 2 * ff), vm(2 * ff, 512), vm(ff, 512),
            vm(8, 2, 32, wide), vm(8, 32, wide), vm(8, 32, wide), vm(8, 32, wide),
            vm(2, 3, 256, 256), vm(2, 16, 64, 256),
            vm(2, 8, rows, ff), vm(2, 2, 2, rows // 2, ff), vm(2, 2, 2, rows, ff), vm(2, rows, ff),
            vm(1, 8, rows, ff), vm(2, 2, 1, rows // 2, ff), vm(2, 2, 1, rows, ff), vm(1, rows, ff),
            vm(4, tok_dev, RCUT), vm(3, 2, tok_dev // 2, most), vm(3, 2, tok_dev, most), vm(tok_dev, width - RCUT),
            vm(2, 4, 8, 128, dtype=F32), vm(8, 128, dtype=F32), vm(2, 4, 8, 128, dtype=F32), vm(7, 8, 128, dtype=F32),
            dma((13,)), dma((2,)), dma((2, 3)), dma((2,)),
            dma((N_SLOT,)), dma((N_SLOT,)), dma((N_SLOT,)), dma((N_SLOT,)), dma((N_SLOT,)), dma((N_SLOT,)),
            dma((7,)), dma((7,)), dma((7,)), dma((7,)), dma((1,)), dma((1,)), dma((16,)), dma((16,)),
            dma((5,)), dma((5,)), dma((3, 4)), dma((3, 4)), dma((2, 5)), dma((2, 5)), dma((2, 5)), dma((2, 5)),
            dma((7,)), dma((7,)), dma((7,)), dma((7,)), pltpu.SemaphoreType.REGULAR,
        ],
        compiler_params=pltpu.CompilerParams(
            collective_id=0, has_side_effects=True, vmem_limit_bytes=63 << 20
        ),
    )(
        tokens, grad_out, ids, slt, counts, score, shared_gate_pre, shared_up_pre,
        shared_w_down, shared_w_gate, shared_w_up, w_gate, w_up, w_down,
    )
    shapes = (
        ((1, width, ff), BF), ((1, width, ff), BF), ((1, ff, width), BF), ((tok_dev, width), BF),
        ((rows, ff), BF), ((rows, ff), BF), ((rows, ff), BF), ((1, tok_dev), F32),
    )
    ggate, gup, gdown, gtok, gsg, gsu, gsd, gscore = pl.pallas_call(
        store_kernel,
        out_shape=tuple(out(*shape, dtype=dtype) for shape, dtype in shapes),
        in_specs=[ANY] * 7,
        out_specs=(ANY,) * 8,
        scratch_shapes=[vm(*shape, dtype=dtype) for shape, dtype in shapes] + [dma((8,)), dma((8,))],
        compiler_params=pltpu.CompilerParams(vmem_limit_bytes=63 << 20),
    )(gtok, gscore, gsg, gsd, ggate, gup, gdown)
    return (gtok, gscore.reshape(tok_dev), gsg, gsu, gsd.T, ggate, gup, gdown)


def solution(mesh):
    placed = (
        P(("grp", "tp"), None),
        P(("grp", "tp"), None),
        P(("grp", "tp")),
        P(("grp", "tp")),
        P(("grp", "tp")),
        P(("grp", "tp"), None),
        P("grp", "tp"),
        P("grp", "tp"),
        P(None, "tp"),
        P(None, "tp"),
        P("tp", None),
        P("grp", None, "tp"),
        P("grp", None, "tp"),
        P("grp", "tp", None),
    )
    return jax.shard_map(
        shards,
        mesh=mesh,
        in_specs=placed,
        out_specs=(
            P(("grp", "tp"), None),
            P(("grp", "tp")),
            P("grp", "tp"),
            P("grp", "tp"),
            P("tp", "grp"),
            P("grp", None, "tp"),
            P("grp", None, "tp"),
            P("grp", "tp", None),
        ),
        check_vma=False,
    )
```

```python
import functools

import jax
import jax.numpy as jnp
from jax import lax
from jax.experimental import pallas as pl
from jax.experimental.pallas import tpu as pltpu
from jax.sharding import PartitionSpec as P

CAP = 4
MESH = pl.DeviceIdType.MESH
BF, F32 = jnp.bfloat16, jnp.float32
ANY = pl.BlockSpec(memory_space=pl.ANY)
VM = pl.BlockSpec(memory_space=pltpu.VMEM)
SM = pl.BlockSpec(memory_space=pltpu.SMEM)
DIRS = (("+", 1), ("-", -1))


def dot_nn(a, b):
    return lax.dot_general(a, b, (((1,), (0,)), ((), ())), preferred_element_type=F32)


def dot_nt(a, b):
    return lax.dot_general(a, b, (((1,), (1,)), ((), ())), preferred_element_type=F32)


def dot_tn(a, b):
    return lax.dot_general(a, b, (((0,), (0,)), ((), ())), preferred_element_type=F32)


class Place:
    def __init__(self):
        self.g = lax.axis_index("grp")
        self.t = lax.axis_index("tp")
        self.xh, self.y = self.g // 4, self.g % 4
        self.xl, self.z, self.c = self.t // 8, (self.t // 2) % 4, self.t % 2

    def chip(self, dx, dz):
        return ((self.xl + dx) % 2) * 4 + (self.z + dz + 4) % 4

    def member(self, dx, dz, other=False):
        core = 1 - self.c if other else self.c
        return self.chip(dx, dz) * 2 + core

    def at(self, dx, dz, other=False):
        return (self.g, self.member(dx, dz, other))

    def group(self, dh, dy):
        return ((self.xh + dh) % 2) * 4 + (self.y + dy + 4) % 4

    def over(self, dh, dy):
        return (self.group(dh, dy), self.t)

    def peer(self, dh, dy):
        return (self.group(dh, dy), (self.t + 8 * dh) % 16)


def greet(targets):
    barrier = pltpu.get_barrier_semaphore()
    for target in targets:
        pl.semaphore_signal(barrier, inc=1, device_id=target, device_id_type=MESH)
    pl.semaphore_wait(barrier, len(targets))


def remote(src, dst, ss, rs, target):
    return pltpu.make_async_remote_copy(
        src_ref=src, dst_ref=dst, send_sem=ss, recv_sem=rs, device_id=target, device_id_type=MESH
    )


ARRIVE = {"xB": (1, 0, None, "B"), "xA0": (1, 0, None, "A")}
for _s, _d in DIRS:
    _h = 0 if _d > 0 else 1
    ARRIVE["zA" + _s] = (0, -_d, None, "A")
    ARRIVE["zB" + _s] = (0, -_d, None, "B")
    ARRIVE["zX" + _s] = (1, -_d, None, "B")
    ARRIVE["hA" + _s] = (0, 2, _h, "A")
    ARRIVE["hB" + _s] = (0, 2, _h, "B")
    ARRIVE["hX" + _s] = (1, 2, _h, "B")
    ARRIVE["xA" + _s] = (1, -_d, None, "A")
    ARRIVE["xh" + _s] = (1, 2, _h, "A")
SLOT = {name: i for i, name in enumerate(ARRIVE)}
N_ICI = len(SLOT)
N_SLOT = 2 * N_ICI + 1


class Gather:
    def __init__(self, place, buf, cut, ss, rs):
        self.p, self.buf, self.cut, self.ss, self.rs = place, buf, cut, ss, rs
        self.rows, self.width = buf.shape[1], buf.shape[2]
        self.sent = {}

    def ref(self, member, half, part):
        rows = pl.ds(0, self.rows) if half is None else pl.ds(half * (self.rows // 2), self.rows // 2)
        cols = {
            None: pl.ds(0, self.width),
            "A": pl.ds(0, self.cut),
            "B": pl.ds(self.cut, self.width - self.cut),
        }[part]
        return self.buf.at[member, rows, cols]

    def send(self, slot, chip, half, part, target):
        ref = self.ref(self.p.member(*chip), half, part)
        copy = remote(ref, ref, self.ss.at[slot], self.rs.at[slot], target)
        copy.start()
        self.sent.setdefault((chip[0], chip[1] % 4), []).append(copy)

    def own(self):
        p, me = self.p, (0, 0)
        for s, d in DIRS:
            self.send(SLOT["zA" + s], me, None, "A", p.at(0, d))
        self.send(SLOT["xB"], me, None, "B", p.at(1, 0))
        self.send(2 * N_ICI, me, None, None, p.at(0, 0, True))

    def own_rest(self):
        p, me = self.p, (0, 0)
        for s, d in DIRS:
            self.send(SLOT["zB" + s], me, None, "B", p.at(0, d))
        self.send(SLOT["xA0"], me, None, "A", p.at(1, 0))

    def take(self, *names):
        for name in names:
            self.take_one(name)

    def take_one(self, name):
        p = self.p
        dx, dz, half, part = ARRIVE[name]
        member = (dx, dz)
        ref = self.ref(p.member(dx, dz), half, part)
        remote(ref, ref, self.ss.at[SLOT[name]], self.rs.at[SLOT[name]], p.at(1, 0)).wait_recv()
        kind, s = name[:2], name[2:]
        if name == "xB":
            for s2, d in DIRS:
                self.send(SLOT["zX" + s2], member, None, "B", p.at(0, d))
        if kind[0] == "z":
            d = 1 if s == "+" else -1
            if kind == "zA":
                self.send(SLOT["xA" + s], member, None, "A", p.at(1, 0))
            self.send(SLOT["h" + kind[1] + s], member, 0 if d > 0 else 1, part, p.at(0, d))
        if kind == "hA":
            self.send(SLOT["xh" + s], member, half, "A", p.at(1, 0))
        self.send(N_ICI + SLOT[name], member, half, part, p.at(0, 0, True))

    def twin(self, *names):
        for name in names:
            if name == "own":
                slot, ref = 2 * N_ICI, self.ref(self.p.member(0, 0, True), None, None)
            else:
                dx, dz, half, part = ARRIVE[name]
                slot, ref = N_ICI + SLOT[name], self.ref(self.p.member(dx, dz, True), half, part)
            remote(ref, ref, self.ss.at[slot], self.rs.at[slot], self.p.at(0, 0, True)).wait_recv()

    def finish(self, chip=None):
        for key in list(self.sent) if chip is None else [(chip[0], chip[1] % 4)]:
            for copy in self.sent.pop(key, []):
                copy.wait_send()


CHIP = ((0, 0), (1, 0), (0, -1), (0, 1), (1, -1), (1, 1), (0, 2), (1, 2))
NEED = (
    ("own",),
    ("xB", "xA0"),
    ("zA+", "zB+"),
    ("zA-", "zB-"),
    ("zX+", "xA+"),
    ("zX-", "xA-"),
    ("hA+", "hA-", "hB+", "hB-"),
    ("hX+", "hX-", "xh+", "xh-"),
)
PEERS = [(dh, dy) for dh in range(2) for dy in range(4) if (dh, dy) != (0, 0)]
MATES = [(dx, dz) for dx in range(2) for dz in range(4) if (dx, dz) != (0, 0)]
CUT = 1152
RCUT = 1024
ORDER = (
    "g2", "Rown", "G0", "r2", "rzA+", "rzA-", "rxB", "M00", "gzB-", "gzA+", "gzA-", "rhA-", "gxA0",
    "rzB+", "rzB-", "rhA+", "gzB+", "rxA-", "gxB", "rzX+", "rzX-", "rxA+", "rxA0", "rxh-", "G2", "G1",
    "ghA-", "Town", "ghA+", "t2", "rxh+", "rhX+", "ghB+", "rhX-", "ghB-", "rhB-", "rhB+", "R0", "R1",
    "Rb", "Rh", "G6", "M03", "G3", "gxA+", "gxh-", "gzX+", "gzX-", "Rs", "Rf", "tzA-", "tzA+", "gxh+",
    "gxA-", "M02", "M01", "tzB+", "tzB-", "G4", "N02", "N01", "M10", "N00", "G5", "L1", "ghX+", "txA0",
    "ghX-", "txB", "M11", "N11", "thA+", "thA-", "N03", "M13", "N13", "N10", "T1", "L0", "G7", "J02",
    "Z10", "D0", "M12", "N12", "J11", "S1", "txA-", "txA+", "tzX-", "tzX+", "T0", "J12", "D1", "Z11",
    "L2", "thB-", "txh-", "thB+", "txh+", "S2", "thX+", "thX-", "J13", "S3", "J00", "T2", "L3", "Z21",
    "D2", "T3", "W0", "X2", "J10", "J01", "Z12", "S0", "J03", "X1", "W0b", "W11", "Z20", "Z31", "Rw0",
    "Rw1", "X3", "Z22", "W10", "D3", "W2", "F2", "F0", "W3",
)


def positions(ids, slots, counts):
    own = jnp.zeros(ids.shape, jnp.int32)
    experts = counts.shape[1]
    for e in range(experts):
        own = own + jnp.where(ids == e, counts[0, e], 0)
    live = (ids < experts) & (slots < own)
    return jnp.where(live, ids * CAP + slots, -1)


def silu_parts(gate):
    sigma = jax.nn.sigmoid(gate)
    return gate * sigma, sigma * (1.0 + gate * (1.0 - sigma))


def kernel(
    tok, grd, ids, slots, counts, score, gpre, upre, wds, wgs, wus, wg, wu, wd,
    gtok, gscore, gsg, gsd, ggate, gup, gdown, TH, RH,
    G, R, TV, SB, RV, dg_v, du_v, wds_v, wgs_v, wus_v, wg_v, wu_v, wd_v, dguT, hidT, acc_gu, acc_d,
    rgu, rguT, rhT, BP, BR, MS, BK, WS, RS, W, WH, WF, WX, WD, DH, DF, DX,
    XA, ZH, ZF, XB, info, mine, QS, QR,
    lsem, tsem, wsem, rsem, gss, grs, tss, trs, rss, rrs, ass, ars, bss, brs, dss, drs, css, crs,
    xss, xrs, zss, zrs, wss, wrs, hss, hrs, iss, irs, qss, qrs, credit,
):
    p = Place()
    g, t, c = p.g, p.t, p.c
    width = gtok.shape[1]
    pieces = ((grd, G.at[t]), (tok, TV.at[0, 0]), (TV.at[0, 0], TH.at[t]), (wds, wds_v), (gpre, dg_v), (upre, du_v),
              (wg.at[0], wg_v), (wu.at[0], wu_v), (wd.at[0], wd_v), (wgs, wgs_v), (wus, wus_v))
    loads = [pltpu.make_async_copy(a, b, lsem.at[i]) for i, (a, b) in enumerate(pieces)]
    for i, copy in enumerate(loads):
        if i != 2:
            copy.start()
    greet(
        [p.at(dx, dz) for dx, dz in MATES]
        + [p.at(0, 0, True)]
        + [p.peer(dh, dy) for dh, dy in PEERS]
        + [p.over(1, 0)]
    )
    gg = Gather(p, G, CUT, gss, grs)
    tg = Gather(p, TH, CUT, tss, trs)
    rg = Gather(p, R, CUT, rss, rrs)
    gathers = {"g": gg, "t": tg, "r": rg}
    sends = []

    def ship(src, dst, ss, rs, target):
        copy = remote(src, dst, ss, rs, target)
        copy.start()
        sends.append(copy)

    def land(ref, ss, rs):
        remote(ref, ref, ss, rs, p.at(0, 0, True)).wait_recv()

    loads[0].wait()
    gg.own()
    loads[1].wait()
    loads[2].start()

    pos = positions(ids[...], slots[...], counts)
    n = SB.shape[0] * 16
    row = lax.broadcasted_iota(jnp.int32, (n, 128), 0)
    pick = pos == (row // 16) * CAP + row % CAP
    scale = jnp.sum(jnp.where(pick, score[...], 0.0), axis=1, keepdims=True)
    pick = pick.astype(F32).astype(BF)
    wide = width // 2
    low = lax.broadcasted_iota(jnp.int32, (n, wide), 0) % 16 < 8
    grad = lax.broadcasted_iota(jnp.int32, (n, wide), 0) % 8 >= CAP
    vals_t = jnp.where(low, dot_nn(pick, TV[0, 0, :, 0:wide]), dot_nn(pick, TV[0, 0, :, wide:])) * scale
    vals_g = jnp.where(low, dot_nn(pick, G[t, :, 0:wide]), dot_nn(pick, G[t, :, wide:]))
    SB[...] = jnp.where(grad, vals_g, vals_t).astype(BF).reshape(SB.shape)
    for i, (dh, dy) in enumerate(PEERS):
        ship(SB.at[p.group(dh, dy)], RV.at[g], ass.at[i], ars.at[i], p.peer(dh, dy))
    RV[pl.ds(g, 1)] = SB[pl.ds(g, 1)]
    which = lax.broadcasted_iota(jnp.int32, (8, 128), 0)
    mine[...] = jnp.where(which == 0, pos.astype(F32), score[...])
    for i, (dx, dz) in enumerate(MATES):
        ship(mine, info.at[dx, (4 - dz) % 4], iss.at[i], irs.at[i], p.at(dx, dz))
    info[0, 0] = mine[...]
    acc_d[...] = jnp.zeros_like(acc_d)
    acc_gu[...] = jnp.zeros_like(acc_gu)

    def cols(i, size):
        return pl.ds(pl.multiple_of(i * size, size), size)

    def rows_own():
        for i, (dh, dy) in enumerate(PEERS):
            land(RV.at[p.group(dh, -dy)], ass.at[i], ars.at[i])
        rows = lax.broadcasted_iota(jnp.int32, (R.shape[1], n), 0)
        at = lax.broadcasted_iota(jnp.int32, (R.shape[1], n), 1)
        base = ((rows % 32) // CAP) * 16 + (rows // 32) * CAP + rows % CAP
        got = RV[...].reshape(n, wide)
        R[t, :, 0:wide] = dot_nn((at == base).astype(F32).astype(BF), got).astype(BF)
        R[t, :, wide:] = dot_nn((at == base + 8).astype(F32).astype(BF), got).astype(BF)
        rg.own()

    def shared_unit(i):
        gg.twin(*NEED[i])
        for k in (3, 4, 5):
            if loads[k] is not None:
                loads[k].wait()
                loads[k] = None
        j = p.chip(*CHIP[i])
        two = pl.ds(2 * j, 2)
        toks = pl.ds(pl.multiple_of(j * 256, 256), 256)
        h = dot_nt(G[two].reshape(256, width), wds_v[...])
        gate, up = dg_v[toks].astype(F32), du_v[toks].astype(F32)
        silu, slope = silu_parts(gate)
        dg, du = h * up * slope, h * silu
        dg_v[toks] = dg.astype(BF)
        du_v[toks] = du.astype(BF)
        dguT[j, 0:256] = dg.T.astype(BF)
        dguT[j, 256:512] = du.T.astype(BF)
        hidT[...] = (silu * up).T.astype(BF)

        def part(k, carry):
            cs = cols(k, 512)
            acc_d[:, cs] += dot_nn(hidT[...], G[two, :, cs].reshape(256, 512))
            return carry

        lax.fori_loop(0, width // 512, part, 0)

    def token_copy(i):
        j = p.chip(*CHIP[i])
        return pltpu.make_async_copy(TH.at[pl.ds(2 * j, 2)], TV.at[i % 2], tsem.at[i % 2])

    def token_load(i):
        for k in (2 * i, 2 * i + 1):
            tg.twin(*NEED[k])
            token_copy(k).start()

    def token_unit(i):
        token_copy(2 * i).wait()
        token_copy(2 * i + 1).wait()
        j, k = p.chip(*CHIP[2 * i]), p.chip(*CHIP[2 * i + 1])

        def part(n, carry):
            cs = cols(n, 512)
            acc_gu[:, cs] += dot_nn(dguT[j], TV[0, :, :, cs].reshape(256, 512)) + dot_nn(
                dguT[k], TV[1, :, :, cs].reshape(256, 512)
            )
            return carry

        lax.fori_loop(0, width // 512, part, 0)

    def r_unit(m):
        if m == 0:
            for i in range(8):
                rg.twin(*NEED[i])
            for k in (6, 7, 8):
                loads[k].wait()
        rin = R[8 * m : 8 * m + 8, 0:32].reshape(256, width)
        rgr = R[8 * m : 8 * m + 8, 32:64].reshape(256, width)
        gate, up = dot_nn(rin, wg_v[...]), dot_nn(rin, wu_v[...])
        h = dot_nt(rgr, wd_v[...])
        silu, slope = silu_parts(gate)
        dg, du = h * up * slope, h * silu
        dgb, dub = dg.astype(BF), du.astype(BF)
        at = pl.ds(m * 256, 256)
        rgu[at, 0:256] = dgb
        rgu[at, 256:512] = dub
        rguT[0:256, at] = dg.T.astype(BF)
        rguT[256:512, at] = du.T.astype(BF)
        rhT[:, at] = (silu * up).T.astype(BF)
        q = jnp.sum(dgb.astype(F32) * gate + dub.astype(F32) * up, axis=1, keepdims=True)
        hi = q.astype(BF).astype(F32)
        lane = lax.broadcasted_iota(jnp.int32, (256, 128), 1)
        tail = jnp.where(lane == 0, hi, jnp.where(lane == 1, q - hi, 0.0)).astype(BF)
        BP[4 * m : 4 * m + 4, :, :, width:] = tail.reshape(4, 2, 32, 128)

    def r_back():
        def part(k, carry):
            cs = cols(k, 512)
            out = dot_nt(rgu[:, 0:256], wg_v[cs]) + dot_nt(rgu[:, 256:512], wu_v[cs])
            BP[:, :, :, cs] = out.astype(BF).reshape(8, 2, 32, 512)
            return carry

        lax.fori_loop(0, width // 512, part, 0)
        ship(BP.at[:, 1 - c], BR, dss.at[0], drs.at[0], p.at(0, 0, True))

    keep = pltpu.make_async_copy(MS.at[g], BK.at[g], lsem.at[11])

    def r_send():
        land(BR, dss.at[0], drs.at[0])

        def part(k, carry):
            one = pl.ds(k, 1)
            BP[one, c] = (BP[one, c].astype(F32) + BR[one].astype(F32)).astype(BF)
            return carry

        lax.fori_loop(0, 8, part, 0)
        r0 = lax.broadcasted_iota(jnp.int32, (256, 256), 0)
        r1 = lax.broadcasted_iota(jnp.int32, (256, 256), 1)
        home, group = (r0 // CAP) % 8, r0 // 32
        held = jnp.where(group // 4 == p.xh, home, (home + 4) % 8)
        turn = (r1 == held * 32 + group * CAP + r0 % CAP).astype(F32).astype(BF)
        MS[...] = dot_nn(turn, BP[:, c].reshape(256, BP.shape[3])).astype(BF).reshape(MS.shape)
        for i, (dh, dy) in enumerate(PEERS):
            ship(MS.at[p.group(dh, dy)], BK.at[g], bss.at[i], brs.at[i], p.peer(dh, dy))
        keep.start()

    def w_copies(k, slot):
        return (
            pltpu.make_async_copy(WS.at[slot, 0], ggate.at[0, cols(k, 256)], wsem.at[slot, 0]),
            pltpu.make_async_copy(WS.at[slot, 1], gup.at[0, cols(k, 256)], wsem.at[slot, 1]),
            pltpu.make_async_copy(WS.at[slot, 2], gdown.at[0, :, cols(k, 256)], wsem.at[slot, 2]),
        )

    def w_load(k, slot):
        return pltpu.make_async_copy(RH.at[:, :, cols(k, 256)], RS.at[slot], rsem.at[slot])

    def w_unit(k, carry):
        slot = k % 2
        w_load(k, slot).wait()

        @pl.when(k + 1 < width // 256)
        def _():
            w_load(k + 1, 1 - slot).start()

        @pl.when(k >= 2)
        def _():
            for copy in w_copies(k - 2, slot):
                copy.wait()

        gu = dot_nn(rguT[...], RS[slot, :, 0:32].reshape(512, 256))
        WS[slot, 0] = gu[0:256].T.astype(BF)
        WS[slot, 1] = gu[256:512].T.astype(BF)
        WS[slot, 2] = dot_nn(rhT[...], RS[slot, :, 32:64].reshape(512, 256)).astype(BF)
        for copy in w_copies(k, slot):
            copy.start()
        return carry

    rows_out = pltpu.make_async_copy(R, RH, lsem.at[12])

    def r_free():
        rg.finish()
        rows_out.wait()
        pl.semaphore_signal(credit, inc=1, device_id=p.at(0, 0, True), device_id_type=MESH)

    half = (pl.ds(0, 160), pl.ds(160, 160))

    def sum_first(V, VH, ss, rs, *dhs):
        for dh in dhs:
            for i, (s, d) in enumerate(DIRS):
                ship(V.at[:, p.group(dh, 2), half[i]], VH.at[dh, i], ss.at[dh, i], rs.at[dh, i], p.over(0, d))

    def sum_second(V, VH, VF, ss, rs, dh):
        for i, (s, d) in enumerate(DIRS):
            land(VH.at[dh, i], ss.at[dh, i], rs.at[dh, i])
            at = p.group(dh, d)
            for a in range(V.shape[0]):
                V[a, at, half[i]] = (V[a, at, half[i]].astype(F32) + VH[dh, i, a].astype(F32)).astype(BF)
            ship(V.at[:, at], VF.at[dh, i], ss.at[dh, 2 + i], rs.at[dh, 2 + i], p.over(0, d))

    def sum_total(V, VF, ss, rs, dh, a):
        return V[a, p.group(dh, 0)].astype(F32) + VF[dh, 0, a].astype(F32) + VF[dh, 1, a].astype(F32)

    def sum_third(V, VF, VX, ss, rs):
        for i in range(2):
            land(VF.at[1, i], ss.at[1, 2 + i], rs.at[1, 2 + i])
        at = p.group(1, 0)
        for a in range(V.shape[0]):
            V[a, at] = sum_total(V, VF, ss, rs, 1, a).astype(BF)
        ship(V.at[:, at], VX, ss.at[0, 4], rs.at[0, 4], p.over(1, 0))

    def sum_last(V, VF, VX, ss, rs):
        for i in range(2):
            land(VF.at[0, i], ss.at[0, 2 + i], rs.at[0, 2 + i])
        land(VX, ss.at[0, 4], rs.at[0, 4])
        return [sum_total(V, VF, ss, rs, 0, a) + VX[a].astype(F32) for a in range(V.shape[0])]

    def turn(acc, V):
        def part(k, carry):
            for a in range(V.shape[0]):
                block = acc[256 * a : 256 * a + 256, cols(k, 640)].T.astype(BF)
                V[a, 2 * k] = block[0:320]
                V[a, 2 * k + 1] = block[320:640]
            return carry

        lax.fori_loop(0, width // 640, part, 0)

    def down_last():
        total = sum_last(WD, DF, DX, hss, hrs)[0]
        gsd[...] = total.astype(BF)

    def weights_last():
        for a, total in enumerate(sum_last(W, WF, WX, wss, wrs)):
            gsg[a] = total.astype(BF)

    seen = set()

    def share(dx, dz):
        if "load" not in seen:
            seen.add("load")
            loads[9].wait()
            loads[10].wait()
        gg.finish((dx, dz))
        j = p.chip(dx, dz)
        toks = pl.ds(pl.multiple_of(j * 256, 256), 256)

        def part(k, carry):
            cs = cols(k, 512)
            out = dot_nt(dg_v[toks], wgs_v[cs]) + dot_nt(du_v[toks], wus_v[cs])
            G[pl.ds(2 * j, 2), :, cs] = out.astype(BF).reshape(2, 128, 512)
            return carry

        lax.fori_loop(0, width // 512, part, 0)

    def swap(dx, dz):
        if "credit" not in seen:
            seen.add("credit")
            pl.semaphore_wait(credit, 1)
        for h in range(2):
            at = 2 * (dx * 4 + dz) + h
            ship(G.at[p.member(dx, dz, True), pl.ds(64 * h, 64)], R.at[at], css.at[at], crs.at[at], p.at(0, 0, True))

    def picked(dx, dz):
        row = lax.broadcasted_iota(jnp.int32, (256, 128), 0)
        want = ((row // 32) * CAP + row % CAP).astype(F32)
        return (want == info[dx, dz, 0:1]) & ((row // CAP) % 8 == p.chip(dx, dz))

    def join(dx, dz):
        if "back" not in seen:
            seen.add("back")
            for i, (dh, dy) in enumerate(PEERS):
                land(BK.at[p.group(dh, -dy)], bss.at[i], brs.at[i])
            keep.wait()
            for i, (ax, az) in enumerate(MATES):
                land(info.at[ax, (4 - az) % 4], iss.at[i], irs.at[i])
            scale = jnp.zeros((256, 1), F32)
            for ax in range(2):
                for az in range(4):
                    scale += jnp.sum(jnp.where(picked(ax, az), info[ax, az, 1:2], 0.0), axis=1, keepdims=True)

            def weigh(k, carry):
                cs = cols(k, 512)
                BK[:, :, cs] = (BK[:, :, cs].reshape(256, 512).astype(F32) * scale).astype(BF).reshape(8, 32, 512)
                return carry

            lax.fori_loop(0, width // 512, weigh, 0)
        slot, me = dx * 4 + dz, p.member(dx, dz)
        pick = picked(dx, dz).astype(F32)
        pickT, pick = pick.T.astype(BF), pick.astype(BF)
        q = dot_tn(BK[:, :, width:].reshape(256, 128), pick)
        QS[dx, dz] = jnp.broadcast_to(q[0:1] + q[1:2], (8, 128))
        if (dx, dz) != (0, 0):
            i = MATES.index((dx, dz))
            ship(QS.at[dx, dz], QR.at[i], qss.at[i], qrs.at[i], p.at(dx, dz))
        for h in range(2):
            land(R.at[2 * slot + h], css.at[2 * slot + h], crs.at[2 * slot + h])

        def part(k, carry):
            cs = cols(k, 512)
            other = R[2 * slot : 2 * slot + 2, :, cs].reshape(128, 512)
            total = dot_nn(pickT, BK[:, :, cs].reshape(256, 512)) + G[me, :, cs].astype(F32) + other.astype(F32)
            G[me, :, cs] = total.astype(BF)
            return carry

        lax.fori_loop(0, width // 512, part, 0)

    colA, colB = pl.ds(0, RCUT), pl.ds(RCUT, width - RCUT)
    rowh = (pl.ds(0, 64), pl.ds(64, 64))

    def cols_of(lane):
        return colA if lane == 2 else colB

    def box(ref, lane, i, rows):
        return ref.at[lane, i, pl.ds(0, rows), pl.ds(0, RCUT if lane == 2 else width - RCUT)]

    def z_first(lane):
        me = p.member(lane % 2, 2)
        for i, (s, d) in enumerate(DIRS):
            ship(G.at[me, rowh[i], cols_of(lane)], box(ZH, lane, i, 64), zss.at[lane, i], zrs.at[lane, i], p.at(0, d))

    def z_second(lane):
        for i, (s, d) in enumerate(DIRS):
            me = p.member(lane % 2, d)
            ref = box(ZH, lane, i, 64)
            land(ref, zss.at[lane, i], zrs.at[lane, i])
            G[me, rowh[i], cols_of(lane)] = (
                G[me, rowh[i], cols_of(lane)].astype(F32) + ref[...].astype(F32)
            ).astype(BF)
            ship(G.at[me, :, cols_of(lane)], box(ZF, lane, i, 128), zss.at[lane, 2 + i], zrs.at[lane, 2 + i], p.at(0, d))

    def z_third(lane):
        for i in range(2):
            land(box(ZF, lane, i, 128), zss.at[lane, 2 + i], zrs.at[lane, 2 + i])
        return (
            G[p.member(lane % 2, 0), :, cols_of(lane)].astype(F32)
            + box(ZF, lane, 0, 128)[...].astype(F32)
            + box(ZF, lane, 1, 128)[...].astype(F32)
        )

    def x_send(dz):
        ship(G.at[p.member(1, dz), :, colA], XA.at[dz], xss.at[dz], xrs.at[dz], p.at(1, 0))

    def x_add(dz):
        land(XA.at[dz], xss.at[dz], xrs.at[dz])
        me = p.member(0, dz)
        G[me, :, colA] = (G[me, :, colA].astype(F32) + XA[dz].astype(F32)).astype(BF)

    def z_cross():
        me = p.member(1, 0)
        G[me, :, colB] = z_third(1).astype(BF)
        ship(G.at[me, :, colB], XB, xss.at[4], xrs.at[4], p.at(1, 0))

    def out_b():
        total = z_third(0)
        land(XB, xss.at[4], xrs.at[4])
        gtok[:, colB] = (total + XB[...].astype(F32)).astype(BF)

    def out_a():
        land(XA.at[0], xss.at[0], xrs.at[0])
        gtok[:, colA] = (z_third(2) + XA[0].astype(F32)).astype(BF)

    def tokens_own():
        loads[2].wait()
        tg.own()

    fixed = {
        "Rown": rows_own, "Town": tokens_own, "g2": gg.own_rest, "t2": tg.own_rest, "r2": rg.own_rest, "Rb": r_back, "Rs": r_send, "Rf": r_free,
        "Rh": rows_out.start,
        "Rw0": lambda: (w_load(0, 0).start(), lax.fori_loop(0, 5, w_unit, 0)), "Rw1": lambda: lax.fori_loop(5, 10, w_unit, 0),
        "D0": lambda: (turn(acc_d, WD), sum_first(WD, DH, hss, hrs, 1, 0)),
        "D1": lambda: (sum_second(WD, DH, DF, hss, hrs, 1), sum_second(WD, DH, DF, hss, hrs, 0)),
        "D2": lambda: sum_third(WD, DF, DX, hss, hrs), "D3": down_last,
        "W0": lambda: (turn(acc_gu, W), sum_first(W, WH, wss, wrs, 1)),
        "W0b": lambda: sum_first(W, WH, wss, wrs, 0),
        "W11": lambda: sum_second(W, WH, WF, wss, wrs, 1), "W10": lambda: sum_second(W, WH, WF, wss, wrs, 0),
        "W2": lambda: sum_third(W, WF, WX, wss, wrs), "W3": weights_last,
        "Z31": z_cross, "F0": out_b, "F2": out_a,
    }
    for step in ORDER:
        if step in fixed:
            fixed[step]()
        elif step[0] in gathers:
            gathers[step[0]].take(step[1:])
        elif step[:2] in ("Z1", "Z2"):
            (z_first if step[1] == "1" else z_second)(int(step[2]))
        else:
            unit = {"G": shared_unit, "L": token_load, "T": token_unit, "R": r_unit, "S": x_send, "X": x_add, "M": share, "N": swap, "J": join}
            unit[step[0]](*(int(k) for k in step[1:]))
    total = QS[0, 0]
    for i in range(len(MATES)):
        land(QR.at[i], qss.at[i], qrs.at[i])
        total = total + QR[i]
    gscore[...] = total[0:1] / score[...]
    for k in (8, 9):
        for copy in w_copies(k, k % 2):
            copy.wait()
    for copy in sends:
        copy.wait_send()
    gg.finish()
    tg.finish()


def store_kernel(gtok, gscore, gsg, gsd, ggate, gup, gdown, *rest):
    parts = (ggate, gup, gdown, gtok, gsg.at[0], gsg.at[1], gsd, gscore)
    outs, held, (first, second) = rest[:8], rest[8:16], rest[16:]
    loads = [pltpu.make_async_copy(a, b, first.at[i]) for i, (a, b) in enumerate(zip(parts, held))]
    stores = [pltpu.make_async_copy(a, b, second.at[i]) for i, (a, b) in enumerate(zip(held, outs))]
    for copy in loads:
        copy.start()
    for load, store in zip(loads, stores):
        load.wait()
        store.start()
    for copy in stores:
        copy.wait()


def shards(
    tokens, grad_out, route_score, expert_ids, slots, counts, shared_gate_pre, shared_up_pre,
    shared_w_gate, shared_w_up, shared_w_down, w_gate, w_up, w_down,
):
    tok_dev, width = tokens.shape
    ff = w_gate.shape[2]
    ids, slt, score = (a.reshape(1, tok_dev) for a in (expert_ids, slots, route_score))
    dma = pltpu.SemaphoreType.DMA
    wide, rows = width + 128, width // 8
    most = max(RCUT, width - RCUT)

    def vm(*shape, dtype=BF):
        return pltpu.VMEM(shape, dtype)

    def out(*shape, dtype=BF):
        return jax.ShapeDtypeStruct(shape, dtype)

    gtok, gscore, gsg, gsd, ggate, gup, gdown, _, _ = pl.pallas_call(
        kernel,
        out_shape=(
            out(tok_dev, width), out(1, tok_dev, dtype=F32), out(2, rows, ff), out(rows, ff),
            out(1, width, ff), out(1, width, ff), out(1, ff, width), out(16, tok_dev, width),
            out(16, 64, width),
        ),
        in_specs=[ANY, ANY, VM, VM, SM, VM] + [ANY] * 8,
        out_specs=(VM, VM, VM, VM, ANY, ANY, ANY, ANY, ANY),
        scratch_shapes=[
            vm(16, tok_dev, width), vm(16, 64, width), vm(2, 2, tok_dev, width),
            vm(8, 16, width // 2), vm(8, 16, width // 2),
            vm(16 * tok_dev, ff), vm(16 * tok_dev, ff),
            vm(ff, width), vm(width, ff), vm(width, ff), vm(width, ff), vm(width, ff), vm(ff, width),
            vm(8, 2 * ff, 256), vm(ff, 256), vm(2 * ff, width, dtype=F32), vm(ff, width, dtype=F32),
            vm(512, 2 * ff), vm(2 * ff, 512), vm(ff, 512),
            vm(8, 2, 32, wide), vm(8, 32, wide), vm(8, 32, wide), vm(8, 32, wide),
            vm(2, 3, 256, 256), vm(2, 16, 64, 256),
            vm(2, 8, rows, ff), vm(2, 2, 2, rows // 2, ff), vm(2, 2, 2, rows, ff), vm(2, rows, ff),
            vm(1, 8, rows, ff), vm(2, 2, 1, rows // 2, ff), vm(2, 2, 1, rows, ff), vm(1, rows, ff),
            vm(4, tok_dev, RCUT), vm(3, 2, tok_dev // 2, most), vm(3, 2, tok_dev, most), vm(tok_dev, width - RCUT),
            vm(2, 4, 8, 128, dtype=F32), vm(8, 128, dtype=F32), vm(2, 4, 8, 128, dtype=F32), vm(7, 8, 128, dtype=F32),
            dma((13,)), dma((2,)), dma((2, 3)), dma((2,)),
            dma((N_SLOT,)), dma((N_SLOT,)), dma((N_SLOT,)), dma((N_SLOT,)), dma((N_SLOT,)), dma((N_SLOT,)),
            dma((7,)), dma((7,)), dma((7,)), dma((7,)), dma((1,)), dma((1,)), dma((16,)), dma((16,)),
            dma((5,)), dma((5,)), dma((3, 4)), dma((3, 4)), dma((2, 5)), dma((2, 5)), dma((2, 5)), dma((2, 5)),
            dma((7,)), dma((7,)), dma((7,)), dma((7,)), pltpu.SemaphoreType.REGULAR,
        ],
        compiler_params=pltpu.CompilerParams(
            collective_id=0, has_side_effects=True, vmem_limit_bytes=63 << 20
        ),
    )(
        tokens, grad_out, ids, slt, counts, score, shared_gate_pre, shared_up_pre,
        shared_w_down, shared_w_gate, shared_w_up, w_gate, w_up, w_down,
    )
    shapes = (
        ((1, width, ff), BF), ((1, width, ff), BF), ((1, ff, width), BF), ((tok_dev, width), BF),
        ((rows, ff), BF), ((rows, ff), BF), ((rows, ff), BF), ((1, tok_dev), F32),
    )
    ggate, gup, gdown, gtok, gsg, gsu, gsd, gscore = pl.pallas_call(
        store_kernel,
        out_shape=tuple(out(*shape, dtype=dtype) for shape, dtype in shapes),
        in_specs=[ANY] * 7,
        out_specs=(ANY,) * 8,
        scratch_shapes=[vm(*shape, dtype=dtype) for shape, dtype in shapes] + [dma((8,)), dma((8,))],
        compiler_params=pltpu.CompilerParams(vmem_limit_bytes=63 << 20),
    )(gtok, gscore, gsg, gsd, ggate, gup, gdown)
    return (gtok, gscore.reshape(tok_dev), gsg, gsu, gsd.T, ggate, gup, gdown)


def solution(mesh):
    placed = (
        P(("grp", "tp"), None),
        P(("grp", "tp"), None),
        P(("grp", "tp")),
        P(("grp", "tp")),
        P(("grp", "tp")),
        P(("grp", "tp"), None),
        P("grp", "tp"),
        P("grp", "tp"),
        P(None, "tp"),
        P(None, "tp"),
        P("tp", None),
        P("grp", None, "tp"),
        P("grp", None, "tp"),
        P("grp", "tp", None),
    )
    return jax.shard_map(
        shards,
        mesh=mesh,
        in_specs=placed,
        out_specs=(
            P(("grp", "tp"), None),
            P(("grp", "tp")),
            P("grp", "tp"),
            P("grp", "tp"),
            P("tp", "grp"),
            P("grp", None, "tp"),
            P("grp", None, "tp"),
            P("grp", "tp", None),
        ),
        check_vma=False,
    )
```

```python
import functools

import jax
import jax.numpy as jnp
from jax import lax
from jax.experimental import pallas as pl
from jax.experimental.pallas import tpu as pltpu
from jax.sharding import PartitionSpec as P

CAP = 4
MESH = pl.DeviceIdType.MESH
BF, F32 = jnp.bfloat16, jnp.float32
ANY = pl.BlockSpec(memory_space=pl.ANY)
VM = pl.BlockSpec(memory_space=pltpu.VMEM)
SM = pl.BlockSpec(memory_space=pltpu.SMEM)
DIRS = (("+", 1), ("-", -1))


def dot_nn(a, b):
    return lax.dot_general(a, b, (((1,), (0,)), ((), ())), preferred_element_type=F32)


def dot_nt(a, b):
    return lax.dot_general(a, b, (((1,), (1,)), ((), ())), preferred_element_type=F32)


def dot_tn(a, b):
    return lax.dot_general(a, b, (((0,), (0,)), ((), ())), preferred_element_type=F32)


class Place:
    def __init__(self):
        self.g = lax.axis_index("grp")
        self.t = lax.axis_index("tp")
        self.xh, self.y = self.g // 4, self.g % 4
        self.xl, self.z, self.c = self.t // 8, (self.t // 2) % 4, self.t % 2

    def chip(self, dx, dz):
        return ((self.xl + dx) % 2) * 4 + (self.z + dz + 4) % 4

    def member(self, dx, dz, other=False):
        core = 1 - self.c if other else self.c
        return self.chip(dx, dz) * 2 + core

    def at(self, dx, dz, other=False):
        return (self.g, self.member(dx, dz, other))

    def group(self, dh, dy):
        return ((self.xh + dh) % 2) * 4 + (self.y + dy + 4) % 4

    def over(self, dh, dy):
        return (self.group(dh, dy), self.t)

    def peer(self, dh, dy):
        return (self.group(dh, dy), (self.t + 8 * dh) % 16)


def greet(targets):
    barrier = pltpu.get_barrier_semaphore()
    for target in targets:
        pl.semaphore_signal(barrier, inc=1, device_id=target, device_id_type=MESH)
    pl.semaphore_wait(barrier, len(targets))


def remote(src, dst, ss, rs, target):
    return pltpu.make_async_remote_copy(
        src_ref=src, dst_ref=dst, send_sem=ss, recv_sem=rs, device_id=target, device_id_type=MESH
    )


ARRIVE = {"xB": (1, 0, None, "B"), "xA0": (1, 0, None, "A")}
for _s, _d in DIRS:
    _h = 0 if _d > 0 else 1
    ARRIVE["zA" + _s] = (0, -_d, None, "A")
    ARRIVE["zB" + _s] = (0, -_d, None, "B")
    ARRIVE["zX" + _s] = (1, -_d, None, "B")
    ARRIVE["hA" + _s] = (0, 2, _h, "A")
    ARRIVE["hB" + _s] = (0, 2, _h, "B")
    ARRIVE["hX" + _s] = (1, 2, _h, "B")
    ARRIVE["xA" + _s] = (1, -_d, None, "A")
    ARRIVE["xh" + _s] = (1, 2, _h, "A")
SLOT = {name: i for i, name in enumerate(ARRIVE)}
N_ICI = len(SLOT)
N_SLOT = 2 * N_ICI + 1


class Gather:
    def __init__(self, place, buf, cut, ss, rs):
        self.p, self.buf, self.cut, self.ss, self.rs = place, buf, cut, ss, rs
        self.rows, self.width = buf.shape[1], buf.shape[2]
        self.sent = {}

    def ref(self, member, half, part):
        rows = pl.ds(0, self.rows) if half is None else pl.ds(half * (self.rows // 2), self.rows // 2)
        cols = {
            None: pl.ds(0, self.width),
            "A": pl.ds(0, self.cut),
            "B": pl.ds(self.cut, self.width - self.cut),
        }[part]
        return self.buf.at[member, rows, cols]

    def send(self, slot, chip, half, part, target):
        ref = self.ref(self.p.member(*chip), half, part)
        copy = remote(ref, ref, self.ss.at[slot], self.rs.at[slot], target)
        copy.start()
        self.sent.setdefault((chip[0], chip[1] % 4), []).append(copy)

    def own(self):
        p, me = self.p, (0, 0)
        for s, d in DIRS:
            self.send(SLOT["zA" + s], me, None, "A", p.at(0, d))
        self.send(SLOT["xB"], me, None, "B", p.at(1, 0))
        self.send(2 * N_ICI, me, None, None, p.at(0, 0, True))

    def own_rest(self):
        p, me = self.p, (0, 0)
        for s, d in DIRS:
            self.send(SLOT["zB" + s], me, None, "B", p.at(0, d))
        self.send(SLOT["xA0"], me, None, "A", p.at(1, 0))

    def take(self, *names):
        for name in names:
            self.take_one(name)

    def take_one(self, name):
        p = self.p
        dx, dz, half, part = ARRIVE[name]
        member = (dx, dz)
        ref = self.ref(p.member(dx, dz), half, part)
        remote(ref, ref, self.ss.at[SLOT[name]], self.rs.at[SLOT[name]], p.at(1, 0)).wait_recv()
        kind, s = name[:2], name[2:]
        if name == "xB":
            for s2, d in DIRS:
                self.send(SLOT["zX" + s2], member, None, "B", p.at(0, d))
        if kind[0] == "z":
            d = 1 if s == "+" else -1
            if kind == "zA":
                self.send(SLOT["xA" + s], member, None, "A", p.at(1, 0))
            self.send(SLOT["h" + kind[1] + s], member, 0 if d > 0 else 1, part, p.at(0, d))
        if kind == "hA":
            self.send(SLOT["xh" + s], member, half, "A", p.at(1, 0))
        self.send(N_ICI + SLOT[name], member, half, part, p.at(0, 0, True))

    def twin(self, *names):
        for name in names:
            if name == "own":
                slot, ref = 2 * N_ICI, self.ref(self.p.member(0, 0, True), None, None)
            else:
                dx, dz, half, part = ARRIVE[name]
                slot, ref = N_ICI + SLOT[name], self.ref(self.p.member(dx, dz, True), half, part)
            remote(ref, ref, self.ss.at[slot], self.rs.at[slot], self.p.at(0, 0, True)).wait_recv()

    def finish(self, chip=None):
        for key in list(self.sent) if chip is None else [(chip[0], chip[1] % 4)]:
            for copy in self.sent.pop(key, []):
                copy.wait_send()


CHIP = ((0, 0), (1, 0), (0, -1), (0, 1), (1, -1), (1, 1), (0, 2), (1, 2))
NEED = (
    ("own",),
    ("xB", "xA0"),
    ("zA+", "zB+"),
    ("zA-", "zB-"),
    ("zX+", "xA+"),
    ("zX-", "xA-"),
    ("hA+", "hA-", "hB+", "hB-"),
    ("hX+", "hX-", "xh+", "xh-"),
)
PEERS = [(dh, dy) for dh in range(2) for dy in range(4) if (dh, dy) != (0, 0)]
MATES = [(dx, dz) for dx in range(2) for dz in range(4) if (dx, dz) != (0, 0)]
CUT = 1152
RCUT = 1024
ORDER = (
    "g2", "Rown", "G0", "r2", "rzA+", "rzA-", "rxB", "M00", "gzB-", "gzA+", "gzA-", "gzB+", "rhA-",
    "gxA0", "rzB+", "rzB-", "rhA+", "rxA-", "gxB", "rzX+", "rzX-", "G2", "rxA+", "G1", "rxA0", "ghA-",
    "Town", "ghA+", "t2", "ghB+", "rxh+", "rxh-", "rhX+", "rhX-", "ghB-", "rhB-", "rhB+", "R0", "R1",
    "Rb", "G6", "M03", "Rh", "G3", "gxA+", "gxh-", "gzX+", "gzX-", "Rs", "Rf", "M01", "tzA-", "gxA-",
    "tzA+", "gxh+", "M02", "tzB+", "tzB-", "G4", "N02", "N01", "N00", "G5", "L1", "M10", "ghX+", "txA0",
    "txB", "M11", "ghX-", "N11", "thA+", "N03", "thA-", "M13", "N13", "N10", "T1", "L0", "G7", "J02",
    "Z10", "D0", "M12", "N12", "J11", "S1", "txA-", "txA+", "tzX-", "tzX+", "T0", "J12", "D1", "Z11",
    "L2", "thB-", "txh-", "thB+", "txh+", "S2", "thX-", "thX+", "J13", "S3", "J00", "T2", "L3", "Z21",
    "D2", "T3", "W0", "X2", "J10", "J01", "Z12", "S0", "J03", "X1", "W0b", "W11", "Z20", "Z31", "Rw0",
    "Rw1", "X3", "Z22", "W10", "D3", "W2", "F2", "F0", "W3",
)


def positions(ids, slots, counts):
    own = jnp.zeros(ids.shape, jnp.int32)
    experts = counts.shape[1]
    for e in range(experts):
        own = own + jnp.where(ids == e, counts[0, e], 0)
    live = (ids < experts) & (slots < own)
    return jnp.where(live, ids * CAP + slots, -1)


def silu_parts(gate):
    sigma = jax.nn.sigmoid(gate)
    return gate * sigma, sigma * (1.0 + gate * (1.0 - sigma))


def kernel(
    tok, grd, ids, slots, counts, score, gpre, upre, wds, wgs, wus, wg, wu, wd,
    gtok, gscore, gsg, gsd, ggate, gup, gdown, TH, RH,
    G, R, TV, SB, RV, dg_v, du_v, wds_v, wgs_v, wus_v, wg_v, wu_v, wd_v, dguT, hidT, acc_gu, acc_d,
    rgu, rguT, rhT, BP, BR, MS, BK, WS, RS, W, WH, WF, WX, WD, DH, DF, DX,
    XA, ZH, ZF, XB, info, mine, QS, QR,
    lsem, tsem, wsem, rsem, gss, grs, tss, trs, rss, rrs, ass, ars, bss, brs, dss, drs, css, crs,
    xss, xrs, zss, zrs, wss, wrs, hss, hrs, iss, irs, qss, qrs, credit,
):
    p = Place()
    g, t, c = p.g, p.t, p.c
    width = gtok.shape[1]
    pieces = ((grd, G.at[t]), (tok, TV.at[0, 0]), (TV.at[0, 0], TH.at[t]), (wds, wds_v), (gpre, dg_v), (upre, du_v),
              (wg.at[0], wg_v), (wu.at[0], wu_v), (wd.at[0], wd_v), (wgs, wgs_v), (wus, wus_v))
    loads = [pltpu.make_async_copy(a, b, lsem.at[i]) for i, (a, b) in enumerate(pieces)]
    for i, copy in enumerate(loads):
        if i != 2:
            copy.start()
    greet(
        [p.at(dx, dz) for dx, dz in MATES]
        + [p.at(0, 0, True)]
        + [p.peer(dh, dy) for dh, dy in PEERS]
        + [p.over(1, 0)]
    )
    gg = Gather(p, G, CUT, gss, grs)
    tg = Gather(p, TH, CUT, tss, trs)
    rg = Gather(p, R, CUT, rss, rrs)
    gathers = {"g": gg, "t": tg, "r": rg}
    sends = []

    def ship(src, dst, ss, rs, target):
        copy = remote(src, dst, ss, rs, target)
        copy.start()
        sends.append(copy)

    def land(ref, ss, rs):
        remote(ref, ref, ss, rs, p.at(0, 0, True)).wait_recv()

    loads[0].wait()
    gg.own()
    loads[1].wait()
    loads[2].start()

    pos = positions(ids[...], slots[...], counts)
    n = SB.shape[0] * 16
    row = lax.broadcasted_iota(jnp.int32, (n, 128), 0)
    pick = pos == (row // 16) * CAP + row % CAP
    scale = jnp.sum(jnp.where(pick, score[...], 0.0), axis=1, keepdims=True)
    pick = pick.astype(F32).astype(BF)
    wide = width // 2
    low = lax.broadcasted_iota(jnp.int32, (n, wide), 0) % 16 < 8
    grad = lax.broadcasted_iota(jnp.int32, (n, wide), 0) % 8 >= CAP
    vals_t = jnp.where(low, dot_nn(pick, TV[0, 0, :, 0:wide]), dot_nn(pick, TV[0, 0, :, wide:])) * scale
    vals_g = jnp.where(low, dot_nn(pick, G[t, :, 0:wide]), dot_nn(pick, G[t, :, wide:]))
    SB[...] = jnp.where(grad, vals_g, vals_t).astype(BF).reshape(SB.shape)
    for i, (dh, dy) in enumerate(PEERS):
        ship(SB.at[p.group(dh, dy)], RV.at[g], ass.at[i], ars.at[i], p.peer(dh, dy))
    RV[pl.ds(g, 1)] = SB[pl.ds(g, 1)]
    which = lax.broadcasted_iota(jnp.int32, (8, 128), 0)
    mine[...] = jnp.where(which == 0, pos.astype(F32), score[...])
    for i, (dx, dz) in enumerate(MATES):
        ship(mine, info.at[dx, (4 - dz) % 4], iss.at[i], irs.at[i], p.at(dx, dz))
    info[0, 0] = mine[...]
    acc_d[...] = jnp.zeros_like(acc_d)
    acc_gu[...] = jnp.zeros_like(acc_gu)

    def cols(i, size):
        return pl.ds(pl.multiple_of(i * size, size), size)

    def rows_own():
        for i, (dh, dy) in enumerate(PEERS):
            land(RV.at[p.group(dh, -dy)], ass.at[i], ars.at[i])
        rows = lax.broadcasted_iota(jnp.int32, (R.shape[1], n), 0)
        at = lax.broadcasted_iota(jnp.int32, (R.shape[1], n), 1)
        base = ((rows % 32) // CAP) * 16 + (rows // 32) * CAP + rows % CAP
        got = RV[...].reshape(n, wide)
        R[t, :, 0:wide] = dot_nn((at == base).astype(F32).astype(BF), got).astype(BF)
        R[t, :, wide:] = dot_nn((at == base + 8).astype(F32).astype(BF), got).astype(BF)
        rg.own()

    def shared_unit(i):
        gg.twin(*NEED[i])
        for k in (3, 4, 5):
            if loads[k] is not None:
                loads[k].wait()
                loads[k] = None
        j = p.chip(*CHIP[i])
        two = pl.ds(2 * j, 2)
        toks = pl.ds(pl.multiple_of(j * 256, 256), 256)
        h = dot_nt(G[two].reshape(256, width), wds_v[...])
        gate, up = dg_v[toks].astype(F32), du_v[toks].astype(F32)
        silu, slope = silu_parts(gate)
        dg, du = h * up * slope, h * silu
        dg_v[toks] = dg.astype(BF)
        du_v[toks] = du.astype(BF)
        dguT[j, 0:256] = dg.T.astype(BF)
        dguT[j, 256:512] = du.T.astype(BF)
        hidT[...] = (silu * up).T.astype(BF)

        def part(k, carry):
            cs = cols(k, 512)
            acc_d[:, cs] += dot_nn(hidT[...], G[two, :, cs].reshape(256, 512))
            return carry

        lax.fori_loop(0, width // 512, part, 0)

    def token_copy(i):
        j = p.chip(*CHIP[i])
        return pltpu.make_async_copy(TH.at[pl.ds(2 * j, 2)], TV.at[i % 2], tsem.at[i % 2])

    def token_load(i):
        for k in (2 * i, 2 * i + 1):
            tg.twin(*NEED[k])
            token_copy(k).start()

    def token_unit(i):
        token_copy(2 * i).wait()
        token_copy(2 * i + 1).wait()
        j, k = p.chip(*CHIP[2 * i]), p.chip(*CHIP[2 * i + 1])

        def part(n, carry):
            cs = cols(n, 512)
            acc_gu[:, cs] += dot_nn(dguT[j], TV[0, :, :, cs].reshape(256, 512)) + dot_nn(
                dguT[k], TV[1, :, :, cs].reshape(256, 512)
            )
            return carry

        lax.fori_loop(0, width // 512, part, 0)

    def r_unit(m):
        if m == 0:
            for i in range(8):
                rg.twin(*NEED[i])
            for k in (6, 7, 8):
                loads[k].wait()
        rin = R[8 * m : 8 * m + 8, 0:32].reshape(256, width)
        rgr = R[8 * m : 8 * m + 8, 32:64].reshape(256, width)
        gate, up = dot_nn(rin, wg_v[...]), dot_nn(rin, wu_v[...])
        h = dot_nt(rgr, wd_v[...])
        silu, slope = silu_parts(gate)
        dg, du = h * up * slope, h * silu
        dgb, dub = dg.astype(BF), du.astype(BF)
        at = pl.ds(m * 256, 256)
        rgu[at, 0:256] = dgb
        rgu[at, 256:512] = dub
        rguT[0:256, at] = dg.T.astype(BF)
        rguT[256:512, at] = du.T.astype(BF)
        rhT[:, at] = (silu * up).T.astype(BF)
        q = jnp.sum(dgb.astype(F32) * gate + dub.astype(F32) * up, axis=1, keepdims=True)
        hi = q.astype(BF).astype(F32)
        lane = lax.broadcasted_iota(jnp.int32, (256, 128), 1)
        tail = jnp.where(lane == 0, hi, jnp.where(lane == 1, q - hi, 0.0)).astype(BF)
        BP[4 * m : 4 * m + 4, :, :, width:] = tail.reshape(4, 2, 32, 128)

    def r_back():
        def part(k, carry):
            cs = cols(k, 512)
            out = dot_nt(rgu[:, 0:256], wg_v[cs]) + dot_nt(rgu[:, 256:512], wu_v[cs])
            BP[:, :, :, cs] = out.astype(BF).reshape(8, 2, 32, 512)
            return carry

        lax.fori_loop(0, width // 512, part, 0)
        ship(BP.at[:, 1 - c], BR, dss.at[0], drs.at[0], p.at(0, 0, True))

    keep = pltpu.make_async_copy(MS.at[g], BK.at[g], lsem.at[11])

    def r_send():
        land(BR, dss.at[0], drs.at[0])

        def part(k, carry):
            one = pl.ds(k, 1)
            BP[one, c] = (BP[one, c].astype(F32) + BR[one].astype(F32)).astype(BF)
            return carry

        lax.fori_loop(0, 8, part, 0)
        r0 = lax.broadcasted_iota(jnp.int32, (256, 256), 0)
        r1 = lax.broadcasted_iota(jnp.int32, (256, 256), 1)
        home, group = (r0 // CAP) % 8, r0 // 32
        held = jnp.where(group // 4 == p.xh, home, (home + 4) % 8)
        turn = (r1 == held * 32 + group * CAP + r0 % CAP).astype(F32).astype(BF)
        MS[...] = dot_nn(turn, BP[:, c].reshape(256, BP.shape[3])).astype(BF).reshape(MS.shape)
        for i, (dh, dy) in enumerate(PEERS):
            ship(MS.at[p.group(dh, dy)], BK.at[g], bss.at[i], brs.at[i], p.peer(dh, dy))
        keep.start()

    def w_copies(k, slot):
        return (
            pltpu.make_async_copy(WS.at[slot, 0], ggate.at[0, cols(k, 256)], wsem.at[slot, 0]),
            pltpu.make_async_copy(WS.at[slot, 1], gup.at[0, cols(k, 256)], wsem.at[slot, 1]),
            pltpu.make_async_copy(WS.at[slot, 2], gdown.at[0, :, cols(k, 256)], wsem.at[slot, 2]),
        )

    def w_load(k, slot):
        return pltpu.make_async_copy(RH.at[:, :, cols(k, 256)], RS.at[slot], rsem.at[slot])

    def w_unit(k, carry):
        slot = k % 2
        w_load(k, slot).wait()

        @pl.when(k + 1 < width // 256)
        def _():
            w_load(k + 1, 1 - slot).start()

        @pl.when(k >= 2)
        def _():
            for copy in w_copies(k - 2, slot):
                copy.wait()

        gu = dot_nn(rguT[...], RS[slot, :, 0:32].reshape(512, 256))
        WS[slot, 0] = gu[0:256].T.astype(BF)
        WS[slot, 1] = gu[256:512].T.astype(BF)
        WS[slot, 2] = dot_nn(rhT[...], RS[slot, :, 32:64].reshape(512, 256)).astype(BF)
        for copy in w_copies(k, slot):
            copy.start()
        return carry

    rows_out = pltpu.make_async_copy(R, RH, lsem.at[12])

    def r_free():
        rg.finish()
        rows_out.wait()
        pl.semaphore_signal(credit, inc=1, device_id=p.at(0, 0, True), device_id_type=MESH)

    half = (pl.ds(0, 160), pl.ds(160, 160))

    def sum_first(V, VH, ss, rs, *dhs):
        for dh in dhs:
            for i, (s, d) in enumerate(DIRS):
                ship(V.at[:, p.group(dh, 2), half[i]], VH.at[dh, i], ss.at[dh, i], rs.at[dh, i], p.over(0, d))

    def sum_second(V, VH, VF, ss, rs, dh):
        for i, (s, d) in enumerate(DIRS):
            land(VH.at[dh, i], ss.at[dh, i], rs.at[dh, i])
            at = p.group(dh, d)
            for a in range(V.shape[0]):
                V[a, at, half[i]] = (V[a, at, half[i]].astype(F32) + VH[dh, i, a].astype(F32)).astype(BF)
            ship(V.at[:, at], VF.at[dh, i], ss.at[dh, 2 + i], rs.at[dh, 2 + i], p.over(0, d))

    def sum_total(V, VF, ss, rs, dh, a):
        return V[a, p.group(dh, 0)].astype(F32) + VF[dh, 0, a].astype(F32) + VF[dh, 1, a].astype(F32)

    def sum_third(V, VF, VX, ss, rs):
        for i in range(2):
            land(VF.at[1, i], ss.at[1, 2 + i], rs.at[1, 2 + i])
        at = p.group(1, 0)
        for a in range(V.shape[0]):
            V[a, at] = sum_total(V, VF, ss, rs, 1, a).astype(BF)
        ship(V.at[:, at], VX, ss.at[0, 4], rs.at[0, 4], p.over(1, 0))

    def sum_last(V, VF, VX, ss, rs):
        for i in range(2):
            land(VF.at[0, i], ss.at[0, 2 + i], rs.at[0, 2 + i])
        land(VX, ss.at[0, 4], rs.at[0, 4])
        return [sum_total(V, VF, ss, rs, 0, a) + VX[a].astype(F32) for a in range(V.shape[0])]

    def turn(acc, V):
        def part(k, carry):
            for a in range(V.shape[0]):
                block = acc[256 * a : 256 * a + 256, cols(k, 640)].T.astype(BF)
                V[a, 2 * k] = block[0:320]
                V[a, 2 * k + 1] = block[320:640]
            return carry

        lax.fori_loop(0, width // 640, part, 0)

    def down_last():
        total = sum_last(WD, DF, DX, hss, hrs)[0]
        gsd[...] = total.astype(BF)

    def weights_last():
        for a, total in enumerate(sum_last(W, WF, WX, wss, wrs)):
            gsg[a] = total.astype(BF)

    seen = set()

    def share(dx, dz):
        if "load" not in seen:
            seen.add("load")
            loads[9].wait()
            loads[10].wait()
        gg.finish((dx, dz))
        j = p.chip(dx, dz)
        toks = pl.ds(pl.multiple_of(j * 256, 256), 256)

        def part(k, carry):
            cs = cols(k, 512)
            out = dot_nt(dg_v[toks], wgs_v[cs]) + dot_nt(du_v[toks], wus_v[cs])
            G[pl.ds(2 * j, 2), :, cs] = out.astype(BF).reshape(2, 128, 512)
            return carry

        lax.fori_loop(0, width // 512, part, 0)

    def swap(dx, dz):
        if "credit" not in seen:
            seen.add("credit")
            pl.semaphore_wait(credit, 1)
        for h in range(2):
            at = 2 * (dx * 4 + dz) + h
            ship(G.at[p.member(dx, dz, True), pl.ds(64 * h, 64)], R.at[at], css.at[at], crs.at[at], p.at(0, 0, True))

    def picked(dx, dz):
        row = lax.broadcasted_iota(jnp.int32, (256, 128), 0)
        want = ((row // 32) * CAP + row % CAP).astype(F32)
        return (want == info[dx, dz, 0:1]) & ((row // CAP) % 8 == p.chip(dx, dz))

    def join(dx, dz):
        if "back" not in seen:
            seen.add("back")
            for i, (dh, dy) in enumerate(PEERS):
                land(BK.at[p.group(dh, -dy)], bss.at[i], brs.at[i])
            keep.wait()
            for i, (ax, az) in enumerate(MATES):
                land(info.at[ax, (4 - az) % 4], iss.at[i], irs.at[i])
            scale = jnp.zeros((256, 1), F32)
            for ax in range(2):
                for az in range(4):
                    scale += jnp.sum(jnp.where(picked(ax, az), info[ax, az, 1:2], 0.0), axis=1, keepdims=True)

            def weigh(k, carry):
                cs = cols(k, 512)
                BK[:, :, cs] = (BK[:, :, cs].reshape(256, 512).astype(F32) * scale).astype(BF).reshape(8, 32, 512)
                return carry

            lax.fori_loop(0, width // 512, weigh, 0)
        slot, me = dx * 4 + dz, p.member(dx, dz)
        pick = picked(dx, dz).astype(F32)
        pickT, pick = pick.T.astype(BF), pick.astype(BF)
        q = dot_tn(BK[:, :, width:].reshape(256, 128), pick)
        QS[dx, dz] = jnp.broadcast_to(q[0:1] + q[1:2], (8, 128))
        if (dx, dz) != (0, 0):
            i = MATES.index((dx, dz))
            ship(QS.at[dx, dz], QR.at[i], qss.at[i], qrs.at[i], p.at(dx, dz))
        for h in range(2):
            land(R.at[2 * slot + h], css.at[2 * slot + h], crs.at[2 * slot + h])

        def part(k, carry):
            cs = cols(k, 512)
            other = R[2 * slot : 2 * slot + 2, :, cs].reshape(128, 512)
            total = dot_nn(pickT, BK[:, :, cs].reshape(256, 512)) + G[me, :, cs].astype(F32) + other.astype(F32)
            G[me, :, cs] = total.astype(BF)
            return carry

        lax.fori_loop(0, width // 512, part, 0)

    colA, colB = pl.ds(0, RCUT), pl.ds(RCUT, width - RCUT)
    rowh = (pl.ds(0, 64), pl.ds(64, 64))

    def cols_of(lane):
        return colA if lane == 2 else colB

    def box(ref, lane, i, rows):
        return ref.at[lane, i, pl.ds(0, rows), pl.ds(0, RCUT if lane == 2 else width - RCUT)]

    def z_first(lane):
        me = p.member(lane % 2, 2)
        for i, (s, d) in enumerate(DIRS):
            ship(G.at[me, rowh[i], cols_of(lane)], box(ZH, lane, i, 64), zss.at[lane, i], zrs.at[lane, i], p.at(0, d))

    def z_second(lane):
        for i, (s, d) in enumerate(DIRS):
            me = p.member(lane % 2, d)
            ref = box(ZH, lane, i, 64)
            land(ref, zss.at[lane, i], zrs.at[lane, i])
            G[me, rowh[i], cols_of(lane)] = (
                G[me, rowh[i], cols_of(lane)].astype(F32) + ref[...].astype(F32)
            ).astype(BF)
            ship(G.at[me, :, cols_of(lane)], box(ZF, lane, i, 128), zss.at[lane, 2 + i], zrs.at[lane, 2 + i], p.at(0, d))

    def z_third(lane):
        for i in range(2):
            land(box(ZF, lane, i, 128), zss.at[lane, 2 + i], zrs.at[lane, 2 + i])
        return (
            G[p.member(lane % 2, 0), :, cols_of(lane)].astype(F32)
            + box(ZF, lane, 0, 128)[...].astype(F32)
            + box(ZF, lane, 1, 128)[...].astype(F32)
        )

    def x_send(dz):
        ship(G.at[p.member(1, dz), :, colA], XA.at[dz], xss.at[dz], xrs.at[dz], p.at(1, 0))

    def x_add(dz):
        land(XA.at[dz], xss.at[dz], xrs.at[dz])
        me = p.member(0, dz)
        G[me, :, colA] = (G[me, :, colA].astype(F32) + XA[dz].astype(F32)).astype(BF)

    def z_cross():
        me = p.member(1, 0)
        G[me, :, colB] = z_third(1).astype(BF)
        ship(G.at[me, :, colB], XB, xss.at[4], xrs.at[4], p.at(1, 0))

    def out_b():
        total = z_third(0)
        land(XB, xss.at[4], xrs.at[4])
        gtok[:, colB] = (total + XB[...].astype(F32)).astype(BF)

    def out_a():
        land(XA.at[0], xss.at[0], xrs.at[0])
        gtok[:, colA] = (z_third(2) + XA[0].astype(F32)).astype(BF)

    def tokens_own():
        loads[2].wait()
        tg.own()

    fixed = {
        "Rown": rows_own, "Town": tokens_own, "g2": gg.own_rest, "t2": tg.own_rest, "r2": rg.own_rest, "Rb": r_back, "Rs": r_send, "Rf": r_free,
        "Rh": rows_out.start,
        "Rw0": lambda: (w_load(0, 0).start(), lax.fori_loop(0, 5, w_unit, 0)), "Rw1": lambda: lax.fori_loop(5, 10, w_unit, 0),
        "D0": lambda: (turn(acc_d, WD), sum_first(WD, DH, hss, hrs, 1, 0)),
        "D1": lambda: (sum_second(WD, DH, DF, hss, hrs, 1), sum_second(WD, DH, DF, hss, hrs, 0)),
        "D2": lambda: sum_third(WD, DF, DX, hss, hrs), "D3": down_last,
        "W0": lambda: (turn(acc_gu, W), sum_first(W, WH, wss, wrs, 1)),
        "W0b": lambda: sum_first(W, WH, wss, wrs, 0),
        "W11": lambda: sum_second(W, WH, WF, wss, wrs, 1), "W10": lambda: sum_second(W, WH, WF, wss, wrs, 0),
        "W2": lambda: sum_third(W, WF, WX, wss, wrs), "W3": weights_last,
        "Z31": z_cross, "F0": out_b, "F2": out_a,
    }
    for step in ORDER:
        if step in fixed:
            fixed[step]()
        elif step[0] in gathers:
            gathers[step[0]].take(step[1:])
        elif step[:2] in ("Z1", "Z2"):
            (z_first if step[1] == "1" else z_second)(int(step[2]))
        else:
            unit = {"G": shared_unit, "L": token_load, "T": token_unit, "R": r_unit, "S": x_send, "X": x_add, "M": share, "N": swap, "J": join}
            unit[step[0]](*(int(k) for k in step[1:]))
    total = QS[0, 0]
    for i in range(len(MATES)):
        land(QR.at[i], qss.at[i], qrs.at[i])
        total = total + QR[i]
    gscore[...] = total[0:1] / score[...]
    for k in (8, 9):
        for copy in w_copies(k, k % 2):
            copy.wait()
    for copy in sends:
        copy.wait_send()
    gg.finish()
    tg.finish()


def store_kernel(gtok, gscore, gsg, gsd, ggate, gup, gdown, *rest):
    parts = (ggate, gup, gdown, gtok, gsg.at[0], gsg.at[1], gsd, gscore)
    outs, held, (first, second) = rest[:8], rest[8:16], rest[16:]
    loads = [pltpu.make_async_copy(a, b, first.at[i]) for i, (a, b) in enumerate(zip(parts, held))]
    stores = [pltpu.make_async_copy(a, b, second.at[i]) for i, (a, b) in enumerate(zip(held, outs))]
    for copy in loads:
        copy.start()
    for load, store in zip(loads, stores):
        load.wait()
        store.start()
    for copy in stores:
        copy.wait()


def shards(
    tokens, grad_out, route_score, expert_ids, slots, counts, shared_gate_pre, shared_up_pre,
    shared_w_gate, shared_w_up, shared_w_down, w_gate, w_up, w_down,
):
    tok_dev, width = tokens.shape
    ff = w_gate.shape[2]
    ids, slt, score = (a.reshape(1, tok_dev) for a in (expert_ids, slots, route_score))
    dma = pltpu.SemaphoreType.DMA
    wide, rows = width + 128, width // 8
    most = max(RCUT, width - RCUT)

    def vm(*shape, dtype=BF):
        return pltpu.VMEM(shape, dtype)

    def out(*shape, dtype=BF):
        return jax.ShapeDtypeStruct(shape, dtype)

    gtok, gscore, gsg, gsd, ggate, gup, gdown, _, _ = pl.pallas_call(
        kernel,
        out_shape=(
            out(tok_dev, width), out(1, tok_dev, dtype=F32), out(2, rows, ff), out(rows, ff),
            out(1, width, ff), out(1, width, ff), out(1, ff, width), out(16, tok_dev, width),
            out(16, 64, width),
        ),
        in_specs=[ANY, ANY, VM, VM, SM, VM] + [ANY] * 8,
        out_specs=(VM, VM, VM, VM, ANY, ANY, ANY, ANY, ANY),
        scratch_shapes=[
            vm(16, tok_dev, width), vm(16, 64, width), vm(2, 2, tok_dev, width),
            vm(8, 16, width // 2), vm(8, 16, width // 2),
            vm(16 * tok_dev, ff), vm(16 * tok_dev, ff),
            vm(ff, width), vm(width, ff), vm(width, ff), vm(width, ff), vm(width, ff), vm(ff, width),
            vm(8, 2 * ff, 256), vm(ff, 256), vm(2 * ff, width, dtype=F32), vm(ff, width, dtype=F32),
            vm(512, 2 * ff), vm(2 * ff, 512), vm(ff, 512),
            vm(8, 2, 32, wide), vm(8, 32, wide), vm(8, 32, wide), vm(8, 32, wide),
            vm(2, 3, 256, 256), vm(2, 16, 64, 256),
            vm(2, 8, rows, ff), vm(2, 2, 2, rows // 2, ff), vm(2, 2, 2, rows, ff), vm(2, rows, ff),
            vm(1, 8, rows, ff), vm(2, 2, 1, rows // 2, ff), vm(2, 2, 1, rows, ff), vm(1, rows, ff),
            vm(4, tok_dev, RCUT), vm(3, 2, tok_dev // 2, most), vm(3, 2, tok_dev, most), vm(tok_dev, width - RCUT),
            vm(2, 4, 8, 128, dtype=F32), vm(8, 128, dtype=F32), vm(2, 4, 8, 128, dtype=F32), vm(7, 8, 128, dtype=F32),
            dma((13,)), dma((2,)), dma((2, 3)), dma((2,)),
            dma((N_SLOT,)), dma((N_SLOT,)), dma((N_SLOT,)), dma((N_SLOT,)), dma((N_SLOT,)), dma((N_SLOT,)),
            dma((7,)), dma((7,)), dma((7,)), dma((7,)), dma((1,)), dma((1,)), dma((16,)), dma((16,)),
            dma((5,)), dma((5,)), dma((3, 4)), dma((3, 4)), dma((2, 5)), dma((2, 5)), dma((2, 5)), dma((2, 5)),
            dma((7,)), dma((7,)), dma((7,)), dma((7,)), pltpu.SemaphoreType.REGULAR,
        ],
        compiler_params=pltpu.CompilerParams(
            collective_id=0, has_side_effects=True, vmem_limit_bytes=63 << 20
        ),
    )(
        tokens, grad_out, ids, slt, counts, score, shared_gate_pre, shared_up_pre,
        shared_w_down, shared_w_gate, shared_w_up, w_gate, w_up, w_down,
    )
    shapes = (
        ((1, width, ff), BF), ((1, width, ff), BF), ((1, ff, width), BF), ((tok_dev, width), BF),
        ((rows, ff), BF), ((rows, ff), BF), ((rows, ff), BF), ((1, tok_dev), F32),
    )
    ggate, gup, gdown, gtok, gsg, gsu, gsd, gscore = pl.pallas_call(
        store_kernel,
        out_shape=tuple(out(*shape, dtype=dtype) for shape, dtype in shapes),
        in_specs=[ANY] * 7,
        out_specs=(ANY,) * 8,
        scratch_shapes=[vm(*shape, dtype=dtype) for shape, dtype in shapes] + [dma((8,)), dma((8,))],
        compiler_params=pltpu.CompilerParams(vmem_limit_bytes=63 << 20),
    )(gtok, gscore, gsg, gsd, ggate, gup, gdown)
    return (gtok, gscore.reshape(tok_dev), gsg, gsu, gsd.T, ggate, gup, gdown)


def solution(mesh):
    placed = (
        P(("grp", "tp"), None),
        P(("grp", "tp"), None),
        P(("grp", "tp")),
        P(("grp", "tp")),
        P(("grp", "tp")),
        P(("grp", "tp"), None),
        P("grp", "tp"),
        P("grp", "tp"),
        P(None, "tp"),
        P(None, "tp"),
        P("tp", None),
        P("grp", None, "tp"),
        P("grp", None, "tp"),
        P("grp", "tp", None),
    )
    return jax.shard_map(
        shards,
        mesh=mesh,
        in_specs=placed,
        out_specs=(
            P(("grp", "tp"), None),
            P(("grp", "tp")),
            P("grp", "tp"),
            P("grp", "tp"),
            P("tp", "grp"),
            P("grp", None, "tp"),
            P("grp", None, "tp"),
            P("grp", "tp", None),
        ),
        check_vma=False,
    )
```
